256 devices in a mesh: dp: 32 (over x_hi, z, core), tensor: 8 (over x_lo, y).
Axes of the slice: x: 4 (x_hi: 2, x_lo: 2; x = x_hi * 2 + x_lo), y: 4, z: 8, core: 2. Of those that a mesh axis runs over, the one named last changes fastest.
Arguments:
- prompt_x: bfloat16 [4096, 5120], P('dp'), may hold values from -6 to 6
- key_matrix: bfloat16 [5120, 1024], P(None, 'tensor'), may hold values from -0.078125 to 0.078125
- value_matrix: bfloat16 [5120, 1024], P(None, 'tensor'), may hold values from -0.078125 to 0.078125
- k_gain: float32 [128], replicated, may hold values from 0.1 to 1.9
- queries: bfloat16 [8192, 8192], P('dp', 'tensor'), may hold values from -64 to 64
- response_keys: bfloat16 [8192, 1024], P('dp', 'tensor'), may hold values from -6 to 6
- response_values: bfloat16 [8192, 1024], P('dp', 'tensor'), may hold values from -6 to 6
- output_gradient: bfloat16 [8192, 8192], P('dp', 'tensor'), may hold values from -96 to 96
- response_counts: int32 [32], replicated, may hold values from 1 to 2, as said below
- slot_prompt: int32 [64], replicated, may hold values from 0 to 15
- prompt_owner: int32 [16], replicated, may hold values from 0 to 15, each once
- prompt_lengths: int32 [16], replicated, may hold values from 64 to 256, as said below
Outputs:
- d_queries: bfloat16 [8192, 8192], P('dp', 'tensor')
- d_resp_keys: bfloat16 [8192, 1024], P('dp', 'tensor')
- d_resp_values: bfloat16 [8192, 1024], P('dp', 'tensor')
- d_prompt_x: bfloat16 [4096, 5120], P('dp', 'tensor')
The draws below stay inside these ranges and needn't reach their ends.
Inputs may be any that keep to these rules, and one draw needn't show every extreme that they name: `response_counts`: some index of dp holds 2 responses. `slot_prompt`: slots at or beyond the count of their index of dp are unused. `prompt_owner`: a permutation; prompt p lies on dp indices prompt_owner[p] * 2 to prompt_owner[p] * 2 + 1, in order. `prompt_lengths`: some prompt has 256 tokens.
All inputs are finite; a program needn't handle non-finite values.
Results may differ from the reference program's by a relative error of at most 0.024.
Values may be sent and summed in bfloat16 or wider, within the bound.
No kernel may reach another device: no remote copies, remote signals or barrier semaphores. Data moves between devices by JAX's collectives and lax.ppermute only.
A program may use at most 64 MiB of HBM per device.

```python
import jax
import jax.numpy as jnp
from jax import lax

MODEL_WIDTH = 5120
QUERY_HEADS = 64
KEY_VALUE_HEADS = 8
HEAD_SIZE = 128
R_CAP = 2
RESPONSE_LENGTH = 128
PROMPT_LENGTH = 256
PROMPTS = 16
PROMPT_ROWS = 4096
SLOTS = 64
RESPONSE_TOKENS = 8192
N_DP = 32


def shared_keys(key):
    value_entries = jax.random.normal(jax.random.fold_in(key, 71), (RESPONSE_TOKENS, KEY_VALUE_HEADS * HEAD_SIZE), jnp.float32)
    return jnp.clip(value_entries, -6.0, 6.0)


def draw_response_keys(key, part):
    base_offset = shared_keys(key)
    return base_offset.astype(jnp.bfloat16)


def draw_queries(key, part):
    key = jax.random.fold_in(key, 6)
    first = jax.random.fold_in(key, 0)
    fresh = jnp.clip(jax.random.normal(first, (RESPONSE_TOKENS, QUERY_HEADS * HEAD_SIZE), jnp.float32), -6.0, 6.0)
    return jnp.clip(fresh, -64.0, 64.0).astype(jnp.bfloat16)


def draw_response_counts(key, part):
    key = jax.random.fold_in(key, 2)
    first, second, third = jax.random.split(key, 3)
    one_draw = jax.random.randint(first, (N_DP,), 1, R_CAP + 1)
    two_draw = jax.random.randint(second, (N_DP,), 1, R_CAP + 1)
    counts = jnp.minimum(one_draw, two_draw)
    busiest = jax.random.randint(third, (), 0, N_DP)
    return counts.at[busiest].set(R_CAP).astype(jnp.int32)


def draw_prompt_lengths(key, part):
    key = jax.random.fold_in(key, 3)
    first, second = jax.random.split(key)
    lengths = jax.random.randint(first, (PROMPTS,), PROMPT_LENGTH // 4, PROMPT_LENGTH + 1)
    longest = jax.random.randint(second, (), 0, PROMPTS)
    return lengths.at[longest].set(PROMPT_LENGTH).astype(jnp.int32)


def with_ends(result, own_key, smallest, largest):
    longest = result.shape.index(max(result.shape))
    spots = []
    for shift in (0, 1):
        where = [jax.random.randint(jax.random.fold_in(own_key, axis), (), 0, length) for axis, length in enumerate(result.shape)]
        where[longest] = (where[longest] + shift) % result.shape[longest]
        spots.append(tuple(where))
    return result.at[spots[0]].set(smallest).at[spots[1]].set(largest)


def block_levels(key, shape, cuts, smallest, high):
    loudness = 1.0
    for position, shards_of in cuts:
        steps = jax.random.uniform(jax.random.fold_in(jax.random.fold_in(key, 6), position), (shards_of,), jnp.float32, smallest / len(cuts), high / len(cuts))
        loudness = loudness * jnp.repeat(jnp.exp(steps), shape[position] // shards_of).reshape((-1,) + (1,) * (len(shape) - 1 - position))
    return loudness


def bell_draw(key, dims, spread, reach, shards=(), kind=jnp.bfloat16):
    level = block_levels(key, dims, shards, -0.22, 0.18) if shards else 1.0
    entries = jax.random.normal(key, dims, jnp.float32) * spread * level
    return jnp.minimum(jnp.maximum(entries, -reach), reach).astype(kind)


def setup_inputs(seed: int = 0) -> dict:
    splits = jax.random.split(jax.random.key(seed), 13)
    prompt_x = bell_draw(splits[0], (PROMPT_ROWS, MODEL_WIDTH), 1.0, 6.0, ((0, 32),))
    key_matrix = bell_draw(splits[1], (MODEL_WIDTH, KEY_VALUE_HEADS * HEAD_SIZE), MODEL_WIDTH ** -0.5, 0.078125, ((1, 8),))
    value_matrix = bell_draw(splits[2], (MODEL_WIDTH, KEY_VALUE_HEADS * HEAD_SIZE), MODEL_WIDTH ** -0.5, 0.078125, ((1, 8),))
    k_gain = jnp.clip(1.0 + 0.18 * jax.random.normal(splits[3], (HEAD_SIZE,), jnp.float32), 0.1, 1.9)
    queries = draw_queries(jax.random.fold_in(splits[12], 71), 0)
    response_keys = draw_response_keys(jax.random.fold_in(splits[12], 71), 0)
    response_values = bell_draw(splits[6], (RESPONSE_TOKENS, KEY_VALUE_HEADS * HEAD_SIZE), 1.0, 6.0, ((0, 32), (1, 8)))
    output_gradient = bell_draw(splits[7], (RESPONSE_TOKENS, QUERY_HEADS * HEAD_SIZE), 16.0, 96.0, ((0, 32), (1, 8)))
    response_counts = draw_response_counts(jax.random.fold_in(splits[12], 71), 0)
    slot_prompt = with_ends(jax.random.randint(splits[9], (SLOTS,), 0, PROMPTS), jax.random.fold_in(splits[9], 1), 0, PROMPTS - 1).astype(jnp.int32)
    prompt_owner = jax.random.permutation(splits[10], PROMPTS).astype(jnp.int32)
    prompt_lengths = draw_prompt_lengths(jax.random.fold_in(splits[12], 71), 0)
    return {"prompt_x": prompt_x, "key_matrix": key_matrix, "value_matrix": value_matrix, "k_gain": k_gain, "queries": queries, "response_keys": response_keys, "response_values": response_values, "output_gradient": output_gradient, "response_counts": response_counts, "slot_prompt": slot_prompt, "prompt_owner": prompt_owner, "prompt_lengths": prompt_lengths}


theta_base = 1000000.0
norm_eps = 1e-06

def rotate_half(value_entries):
    half = value_entries.shape[-1] // 2
    return jnp.concatenate([-value_entries[..., half:], value_entries[..., :half]], axis=-1)

def key_prep(raw_keys, k_gain, positions):
    rows = raw_keys.shape[0]
    heads = raw_keys.reshape(rows, -1, HEAD_SIZE)
    scale_inv = lax.rsqrt(lax.optimization_barrier(jnp.mean(heads * heads, axis=-1, keepdims=True)) + norm_eps)
    normed = heads * scale_inv * k_gain
    freqs = theta_base ** (-jnp.arange(HEAD_SIZE // 2, dtype=jnp.float32) * 2.0 / HEAD_SIZE)
    angles = positions.astype(jnp.float32)[:, None] * freqs[None, :]
    angles = jnp.concatenate([angles, angles], axis=-1)[:, None, :]
    rotated = normed * jnp.cos(angles) + rotate_half(normed) * jnp.sin(angles)
    return rotated.reshape(rows, -1)

def slot_grads(queries, output_gradient, prompt_key_rows, prompt_value_rows, own_keys, own_values, length):
    single_float = jnp.float32
    scale = HEAD_SIZE ** (-0.5)
    plen = prompt_key_rows.shape[0]
    rlen = queries.shape[0]
    qf = queries.astype(single_float)
    gf = output_gradient.astype(single_float)
    prefix_key_block = prompt_key_rows.astype(single_float)
    prefix_value_block = prompt_value_rows.astype(single_float)
    response_key_block = own_keys.astype(single_float)
    response_value_block = own_values.astype(single_float)
    s_pre = jnp.einsum('thgd,jhd->hgtj', qf, prefix_key_block) * scale
    s_own = jnp.einsum('thgd,jhd->hgtj', qf, response_key_block) * scale
    visible = jnp.arange(plen) < length
    s_pre = jnp.where(visible, s_pre, -jnp.inf)
    causal = jnp.arange(rlen)[None, :] <= jnp.arange(rlen)[:, None]
    s_own = jnp.where(causal, s_own, -jnp.inf)
    top = jnp.maximum(lax.optimization_barrier(jnp.max(s_pre, axis=-1, keepdims=True)), lax.optimization_barrier(jnp.max(s_own, axis=-1, keepdims=True)))
    e_pre = jnp.exp(s_pre - top)
    e_own = jnp.exp(s_own - top)
    total = lax.optimization_barrier(jnp.sum(e_pre, axis=-1, keepdims=True)) + lax.optimization_barrier(jnp.sum(e_own, axis=-1, keepdims=True))
    p_pre = e_pre / total
    p_own = e_own / total
    pb_pre = p_pre.astype(jnp.bfloat16).astype(single_float)
    pb_own = p_own.astype(jnp.bfloat16).astype(single_float)
    attn_out = jnp.einsum('hgtj,jhd->hgtd', pb_pre, prefix_value_block) + jnp.einsum('hgtj,jhd->hgtd', pb_own, response_value_block)
    delta = jnp.einsum('thgd,hgtd->hgt', gf, attn_out)[..., None]
    dp_pre = jnp.einsum('thgd,jhd->hgtj', gf, prefix_value_block)
    dp_own = jnp.einsum('thgd,jhd->hgtj', gf, response_value_block)
    ds_pre = (p_pre * (dp_pre - delta) * scale).astype(jnp.bfloat16).astype(single_float)
    ds_own = (p_own * (dp_own - delta) * scale).astype(jnp.bfloat16).astype(single_float)
    d_q = jnp.einsum('hgtj,jhd->thgd', ds_pre, prefix_key_block) + jnp.einsum('hgtj,jhd->thgd', ds_own, response_key_block)
    d_rk = jnp.einsum('hgtj,thgd->jhd', ds_own, qf)
    d_rv = jnp.einsum('hgtj,thgd->jhd', pb_own, gf)
    d_pk = jnp.einsum('hgtj,thgd->jhd', ds_pre, qf)
    d_pv = jnp.einsum('hgtj,thgd->jhd', pb_pre, gf)
    return (d_q, d_rk, d_rv, d_pk, d_pv)

def reference(prompt_x, key_matrix, value_matrix, k_gain, queries, response_keys, response_values, output_gradient, response_counts, slot_prompt, prompt_owner, prompt_lengths):
    single_float = jnp.float32
    bf16 = jnp.bfloat16
    rows = prompt_x.shape[0]
    query_groups = QUERY_HEADS // KEY_VALUE_HEADS
    key_value_width = KEY_VALUE_HEADS * HEAD_SIZE
    positions = (jnp.arange(rows) % PROMPT_LENGTH).astype(jnp.int32)
    raw_keys = jnp.dot(prompt_x, key_matrix, preferred_element_type=single_float)
    prompt_value_rows = jnp.dot(prompt_x, value_matrix, preferred_element_type=single_float).astype(bf16)
    keys_float, prep_back = jax.vjp(lambda raw: key_prep(raw, k_gain, positions), raw_keys)
    prompt_key_rows = keys_float.astype(bf16)

    def one_slot(carry, slot):
        key_sum, value_sum = carry
        device = slot // R_CAP
        live = slot % R_CAP < response_counts[device]
        prompt = slot_prompt[slot]
        start_offset = (prompt_owner[prompt] * PROMPT_LENGTH).astype(jnp.int32)
        length = prompt_lengths[prompt]
        base_offset = (slot * RESPONSE_LENGTH).astype(jnp.int32)
        prefix_key_block = lax.dynamic_slice_in_dim(prompt_key_rows, start_offset, PROMPT_LENGTH, 0).reshape(PROMPT_LENGTH, KEY_VALUE_HEADS, HEAD_SIZE)
        prefix_value_block = lax.dynamic_slice_in_dim(prompt_value_rows, start_offset, PROMPT_LENGTH, 0).reshape(PROMPT_LENGTH, KEY_VALUE_HEADS, HEAD_SIZE)
        query_block = lax.dynamic_slice_in_dim(queries, base_offset, RESPONSE_LENGTH, 0).reshape(RESPONSE_LENGTH, KEY_VALUE_HEADS, query_groups, HEAD_SIZE)
        group_index = lax.dynamic_slice_in_dim(output_gradient, base_offset, RESPONSE_LENGTH, 0).reshape(RESPONSE_LENGTH, KEY_VALUE_HEADS, query_groups, HEAD_SIZE)
        response_key_block = lax.dynamic_slice_in_dim(response_keys, base_offset, RESPONSE_LENGTH, 0).reshape(RESPONSE_LENGTH, KEY_VALUE_HEADS, HEAD_SIZE)
        response_value_block = lax.dynamic_slice_in_dim(response_values, base_offset, RESPONSE_LENGTH, 0).reshape(RESPONSE_LENGTH, KEY_VALUE_HEADS, HEAD_SIZE)

        def compute(unused):
            return slot_grads(query_block, group_index, prefix_key_block, prefix_value_block, response_key_block, response_value_block, length)

        def skip(unused):
            return (jnp.zeros((RESPONSE_LENGTH, KEY_VALUE_HEADS, query_groups, HEAD_SIZE), single_float), jnp.zeros((RESPONSE_LENGTH, KEY_VALUE_HEADS, HEAD_SIZE), single_float), jnp.zeros((RESPONSE_LENGTH, KEY_VALUE_HEADS, HEAD_SIZE), single_float), jnp.zeros((PROMPT_LENGTH, KEY_VALUE_HEADS, HEAD_SIZE), single_float), jnp.zeros((PROMPT_LENGTH, KEY_VALUE_HEADS, HEAD_SIZE), single_float))
        d_q, d_rk, d_rv, d_pk, d_pv = lax.cond(live, compute, skip, 0)
        key_sum = lax.dynamic_update_slice_in_dim(key_sum, lax.dynamic_slice_in_dim(key_sum, start_offset, PROMPT_LENGTH, 0) + d_pk.reshape(PROMPT_LENGTH, key_value_width), start_offset, 0)
        value_sum = lax.dynamic_update_slice_in_dim(value_sum, lax.dynamic_slice_in_dim(value_sum, start_offset, PROMPT_LENGTH, 0) + d_pv.reshape(PROMPT_LENGTH, key_value_width), start_offset, 0)
        outputs = (d_q.reshape(RESPONSE_LENGTH, QUERY_HEADS * HEAD_SIZE).astype(bf16), d_rk.reshape(RESPONSE_LENGTH, key_value_width).astype(bf16), d_rv.reshape(RESPONSE_LENGTH, key_value_width).astype(bf16))
        return ((key_sum, value_sum), outputs)
    start_sums = (jnp.zeros((rows, key_value_width), single_float), jnp.zeros((rows, key_value_width), single_float))
    (key_grads, value_grads), (d_q, d_rk, d_rv) = lax.scan(one_slot, start_sums, jnp.arange(SLOTS, dtype=jnp.int32))
    raw_grads = prep_back(key_grads)[0].astype(bf16)
    value_grads_b = value_grads.astype(bf16)
    d_prompt = jnp.dot(raw_grads, key_matrix.T, preferred_element_type=single_float) + jnp.dot(value_grads_b, value_matrix.T, preferred_element_type=single_float)
    return (d_q.reshape(RESPONSE_TOKENS, QUERY_HEADS * HEAD_SIZE), d_rk.reshape(RESPONSE_TOKENS, key_value_width), d_rv.reshape(RESPONSE_TOKENS, key_value_width), d_prompt.astype(bf16))
```

```python
import functools

import jax
import jax.numpy as jnp
import numpy as np
from jax import lax
from jax.experimental import pallas as pl
from jax.experimental.pallas import tpu as pltpu
from jax.sharding import Mesh
from jax.sharding import PartitionSpec as P

HEAD = 128
R_CAP = 2
RLEN = 128
PLEN = 256
HALF = 128
CHIPS = 16
CORES = 2
PIECE = HALF // CHIPS
UNIT = 2 * PIECE
WIDTH = 5120
TENSOR = 8
COLS = WIDTH // TENSOR
GROUPS = 8
SCALE = HEAD ** (-0.5)
EXP2_SCALE = SCALE * float(np.log2(np.e))
EPS = 1e-06
f32 = jnp.float32
bf16 = jnp.bfloat16
SPREAD = ("x_hi", "z")
SMEM = pl.BlockSpec(memory_space=pltpu.SMEM)


def rope_tables():
    freqs = 1000000.0 ** (-np.arange(HEAD // 2, dtype=np.float64) * 2.0 / HEAD)
    angles = np.arange(PLEN, dtype=np.float64)[:, None] * freqs[None, :]
    cos, sin = np.cos(angles), np.sin(angles)
    shape = (CORES, HALF, HEAD)
    c = np.concatenate([cos, cos], axis=1).astype(np.float32).reshape(shape)
    s = np.concatenate([-sin, sin], axis=1).astype(np.float32).reshape(shape)
    return c, s


def swap_halves(u):
    return pltpu.roll(u, HEAD // 2, 1)


def to_units(keys, values):
    n = keys.shape[0] // PIECE
    return jnp.concatenate(
        [keys.reshape(n, PIECE, HEAD), values.reshape(n, PIECE, HEAD)], axis=1
    )


def from_units(units):
    u = units.astype(f32)
    n = u.shape[0]
    return u[:, :PIECE].reshape(n * PIECE, HEAD), u[:, PIECE:].reshape(n * PIECE, HEAD)


def dot_nn(a, b):
    return lax.dot_general(a, b, (((1,), (0,)), ((), ())), preferred_element_type=f32)


def dot_nt(a, b):
    return lax.dot_general(a, b, (((1,), (1,)), ((), ())), preferred_element_type=f32)


def project_kernel(steps, core_ref, x_ref, wk_ref, wv_ref, gain_ref, c_ref, s_ref, kv_ref, raw_ref, acc):
    step = pl.program_id(0)
    w = jnp.concatenate([wk_ref[...], wv_ref[...]], axis=1)
    part = dot_nn(x_ref[...], w)

    @pl.when(step == 0)
    def _():
        acc[...] = part

    @pl.when(step > 0)
    def _():
        acc[...] += part

    @pl.when(step == steps - 1)
    def _():
        core = core_ref[0]
        raw = acc[:, :HEAD]
        raw_ref[...] = raw
        inv = lax.rsqrt(jnp.mean(raw * raw, axis=-1, keepdims=True) + EPS)
        u = raw * inv * gain_ref[...]
        keys = u * c_ref[core] + swap_halves(u) * s_ref[core]
        kv_ref[...] = to_units(keys, acc[:, HEAD:]).astype(bf16)


def project(core, x, wk, wv, gain, c, s):
    steps = 4
    tk = WIDTH // steps
    whole = lambda *shape: pl.BlockSpec(shape, lambda i: (0,) * len(shape))
    return pl.pallas_call(
        functools.partial(project_kernel, steps),
        grid=(steps,),
        in_specs=[
            SMEM,
            pl.BlockSpec((HALF, tk), lambda i: (0, i)),
            pl.BlockSpec((tk, HEAD), lambda i: (i, 0)),
            pl.BlockSpec((tk, HEAD), lambda i: (i, 0)),
            whole(1, HEAD),
            whole(CORES, HALF, HEAD),
            whole(CORES, HALF, HEAD),
        ],
        out_specs=[whole(CHIPS, UNIT, HEAD), whole(HALF, HEAD)],
        out_shape=[
            jax.ShapeDtypeStruct((CHIPS, UNIT, HEAD), bf16),
            jax.ShapeDtypeStruct((HALF, HEAD), f32),
        ],
        scratch_shapes=[pltpu.VMEM((HALF, 2 * HEAD), f32)],
        compiler_params=pltpu.CompilerParams(vmem_limit_bytes=16 << 20),
        cost_estimate=pl.CostEstimate(flops=2 * HALF * WIDTH * 256, bytes_accessed=4 << 20, transcendentals=0),
        name="project",
    )(core, x, wk, wv, gain, c, s)


def select_kernel(core_ref, slot_prompt_ref, owner_ref, mine_ref, other_ref, out_ref):
    core = core_ref[0]
    for chip in range(CHIPS):
        for r in range(R_CAP):
            q = owner_ref[slot_prompt_ref[chip * CORES * R_CAP + core * R_CAP + r]]
            out_ref[chip, r, 0] = mine_ref[q]
            out_ref[chip, r, 1] = other_ref[q]


def select(core, slot_prompt, owner, mine, other):
    vmem = pl.BlockSpec(memory_space=pltpu.VMEM)
    return pl.pallas_call(
        select_kernel,
        in_specs=[SMEM, SMEM, SMEM, vmem, vmem],
        out_specs=vmem,
        out_shape=jax.ShapeDtypeStruct((CHIPS, R_CAP, 2, UNIT, HEAD), bf16),
        compiler_params=pltpu.CompilerParams(vmem_limit_bytes=8 << 20),
        name="select",
    )(core, slot_prompt, owner, mine, other)


def attend_kernel(
    ids_ref, counts_ref, slot_prompt_ref, lengths_ref,
    kv_ref, q_ref, g_ref, rk_ref, rv_ref,
    dq_ref, drk_ref, drv_ref, grads_ref,
    ds_s, pb_s,
):
    slot = pl.program_id(0)
    core, dp = ids_ref[0], ids_ref[1]
    live = slot < counts_ref[dp]

    @pl.when(live)
    def _():
        length = lengths_ref[slot_prompt_ref[dp * R_CAP + slot]]
        ka, va = from_units(kv_ref[:, 0, 0])
        kb, vb = from_units(kv_ref[:, 0, 1])
        keys = jnp.concatenate([ka.astype(bf16), kb.astype(bf16), rk_ref[...]], axis=0)
        values = jnp.concatenate([va.astype(bf16), vb.astype(bf16), rv_ref[...]], axis=0)
        row = lax.broadcasted_iota(jnp.int32, (HALF, RLEN), 0)
        query = lax.broadcasted_iota(jnp.int32, (HALF, RLEN), 1)
        seen = jnp.concatenate(
            [
                row + core * HALF < length,
                row + (1 - core) * HALF < length,
                row <= query,
            ],
            axis=0,
        )
        for h in range(GROUPS):
            cols = slice(h * HEAD, (h + 1) * HEAD)
            qh = q_ref[:, cols]
            gh = g_ref[:, cols]
            st = jnp.where(seen, dot_nt(keys, qh), -jnp.inf)
            dpt = dot_nt(values, gh)
            top = jnp.max(st, axis=0, keepdims=True)
            e = jnp.exp2((st - top) * EXP2_SCALE)
            inv = 1.0 / jnp.sum(e, axis=0, keepdims=True)
            p = e * inv
            pb = p.astype(bf16)
            pb_s[:, cols] = pb
            delta = jnp.sum(pb.astype(f32) * dpt, axis=0, keepdims=True)
            ds_s[:, cols] = (p * ((dpt - delta) * SCALE)).astype(bf16)
        q_rows = jnp.concatenate([q_ref[:, h * HEAD:(h + 1) * HEAD] for h in range(GROUPS)], axis=0)
        g_rows = jnp.concatenate([g_ref[:, h * HEAD:(h + 1) * HEAD] for h in range(GROUPS)], axis=0)
        dk = dot_nn(ds_s[...], q_rows)
        dv = dot_nn(pb_s[...], g_rows)
        grads_ref[:, 0, 0] = to_units(dk[:HALF], dv[:HALF]).astype(bf16)
        grads_ref[:, 0, 1] = to_units(dk[HALF:PLEN], dv[HALF:PLEN]).astype(bf16)
        drk_ref[...] = dk[PLEN:].astype(bf16)
        drv_ref[...] = dv[PLEN:].astype(bf16)
        keys_t = keys.T
        for h in range(GROUPS):
            cols = slice(h * HEAD, (h + 1) * HEAD)
            dq_ref[:, cols] = dot_nn(keys_t, ds_s[:, cols]).T.astype(bf16)

    @pl.when(jnp.logical_not(live))
    def _():
        grads_ref[...] = jnp.zeros_like(grads_ref)
        drk_ref[...] = jnp.zeros_like(drk_ref)
        drv_ref[...] = jnp.zeros_like(drv_ref)
        dq_ref[...] = jnp.zeros_like(dq_ref)


def attend(ids, counts, slot_prompt, lengths, kv, q, g, rk, rv):
    width = GROUPS * HEAD
    rows = lambda n: pl.BlockSpec((RLEN, n), lambda i: (i, 0))
    units = pl.BlockSpec((CHIPS, 1, 2, UNIT, HEAD), lambda i: (0, i, 0, 0, 0))
    return pl.pallas_call(
        attend_kernel,
        grid=(R_CAP,),
        in_specs=[SMEM] * 4 + [units, rows(width), rows(width), rows(HEAD), rows(HEAD)],
        out_specs=[rows(width), rows(HEAD), rows(HEAD), units],
        out_shape=[
            jax.ShapeDtypeStruct((R_CAP * RLEN, width), bf16),
            jax.ShapeDtypeStruct((R_CAP * RLEN, HEAD), bf16),
            jax.ShapeDtypeStruct((R_CAP * RLEN, HEAD), bf16),
            jax.ShapeDtypeStruct((CHIPS, R_CAP, 2, UNIT, HEAD), bf16),
        ],
        scratch_shapes=[
            pltpu.VMEM((PLEN + RLEN, width), bf16),
            pltpu.VMEM((PLEN + RLEN, width), bf16),
        ],
        compiler_params=pltpu.CompilerParams(vmem_limit_bytes=32 << 20),
        cost_estimate=pl.CostEstimate(flops=10 * 2 * 384 * 1024 * 128, bytes_accessed=3 << 20, transcendentals=2 * 384 * 1024),
        name="attend",
    )(ids, counts, slot_prompt, lengths, kv, q, g, rk, rv)


def collect_kernel(core_ref, slot_prompt_ref, owner_ref, got_ref, mine_ref, other_ref, acc):
    core = core_ref[0]
    acc[...] = jnp.zeros_like(acc)
    for chip in range(CHIPS):
        for r in range(R_CAP):
            q = owner_ref[slot_prompt_ref[chip * CORES * R_CAP + core * R_CAP + r]]
            acc[q] += got_ref[chip, r].astype(f32)
    mine_ref[...] = acc[:, 0]
    other_ref[...] = acc[:, 1].astype(bf16)


def collect(core, slot_prompt, owner, got):
    vmem = pl.BlockSpec(memory_space=pltpu.VMEM)
    return pl.pallas_call(
        collect_kernel,
        in_specs=[SMEM, SMEM, SMEM, vmem],
        out_specs=[vmem, vmem],
        out_shape=[
            jax.ShapeDtypeStruct((CHIPS, UNIT, HEAD), f32),
            jax.ShapeDtypeStruct((CHIPS, UNIT, HEAD), bf16),
        ],
        scratch_shapes=[pltpu.VMEM((CHIPS, 2, UNIT, HEAD), f32)],
        compiler_params=pltpu.CompilerParams(vmem_limit_bytes=8 << 20),
        name="collect",
    )(core, slot_prompt, owner, got)


def unproject_kernel(core_ref, units_ref, raw_ref, gain_ref, c_ref, s_ref, wk_ref, wv_ref, out_ref, grads):
    @pl.when(pl.program_id(0) == 0)
    def _():
        core = core_ref[0]
        dk, dv = from_units(units_ref[...])
        raw = raw_ref[...]
        inv = lax.rsqrt(jnp.mean(raw * raw, axis=-1, keepdims=True) + EPS)
        du = dk * c_ref[core] + swap_halves(dk * s_ref[core])
        dn = du * gain_ref[...]
        dot = jnp.mean(raw * dn, axis=-1, keepdims=True)
        grads[:, :HEAD] = (inv * (dn - raw * (inv * inv * dot))).astype(bf16)
        grads[:, HEAD:] = dv.astype(bf16)

    w = jnp.concatenate([wk_ref[...], wv_ref[...]], axis=1)
    out_ref[0] = dot_nt(grads[...], w).astype(bf16)


def unproject(core, units, raw, gain, c, s, wk, wv):
    whole = lambda *shape: pl.BlockSpec(shape, lambda i: (0,) * len(shape))
    return pl.pallas_call(
        unproject_kernel,
        grid=(TENSOR,),
        in_specs=[
            SMEM,
            whole(CHIPS, UNIT, HEAD),
            whole(HALF, HEAD),
            whole(1, HEAD),
            whole(CORES, HALF, HEAD),
            whole(CORES, HALF, HEAD),
            pl.BlockSpec((COLS, HEAD), lambda i: (i, 0)),
            pl.BlockSpec((COLS, HEAD), lambda i: (i, 0)),
        ],
        out_specs=pl.BlockSpec((1, HALF, COLS), lambda i: (i, 0, 0)),
        out_shape=jax.ShapeDtypeStruct((TENSOR, HALF, COLS), bf16),
        scratch_shapes=[pltpu.VMEM((HALF, 2 * HEAD), bf16)],
        compiler_params=pltpu.CompilerParams(vmem_limit_bytes=16 << 20),
        cost_estimate=pl.CostEstimate(flops=2 * HALF * WIDTH * 256, bytes_accessed=4 << 20, transcendentals=0),
        name="unproject",
    )(core, units, raw, gain, c, s, wk, wv)


def spread(x):
    return lax.all_to_all(x, SPREAD, 0, 0, tiled=True)


def swap_cores(x):
    return lax.ppermute(x, "core", [(0, 1), (1, 0)])


def on_device(
    prompt_x, key_matrix, value_matrix, k_gain, queries, response_keys, response_values,
    output_gradient, response_counts, slot_prompt, prompt_owner, prompt_lengths,
):
    core_index = lax.axis_index("core").astype(jnp.int32)
    dp_index = lax.axis_index(("x_hi", "z", "core")).astype(jnp.int32)
    ids = jnp.stack([core_index, dp_index])
    c, s = rope_tables()
    gain = k_gain.reshape(1, HEAD)
    with jax.named_scope("keys_out"):
        kv, raw = project(ids, prompt_x, key_matrix, value_matrix, gain, c, s)
        mine = spread(kv)
        other = swap_cores(mine)
        needed = spread(select(ids, slot_prompt, prompt_owner, mine, other))
    with jax.named_scope("attention"):
        dq, drk, drv, grads = attend(
            ids, response_counts, slot_prompt, prompt_lengths,
            needed, queries, output_gradient, response_keys, response_values,
        )
    with jax.named_scope("grads_back"):
        sum_mine, sum_other = collect(ids, slot_prompt, prompt_owner, spread(grads))
        units = (sum_mine + swap_cores(sum_other).astype(f32)).astype(bf16)
        units = spread(units)
    with jax.named_scope("input_grad"):
        shares = unproject(ids, units, raw, gain, c, s, key_matrix, value_matrix)
        shares = lax.all_to_all(shares, ("x_lo", "y"), 0, 0, tiled=True)
        d_prompt = jnp.sum(shares.astype(f32), axis=0).astype(bf16)
    return dq, drk, drv, d_prompt


def solution(mesh):
    fine = Mesh(mesh.devices.reshape(2, 8, 2, 2, 4), ("x_hi", "z", "core", "x_lo", "y"))
    dp, tensor = ("x_hi", "z", "core"), ("x_lo", "y")
    both = P(dp, tensor)
    return jax.shard_map(
        on_device,
        mesh=fine,
        in_specs=(P(dp, None), P(None, tensor), P(None, tensor), P(), both, both, both, both, P(), P(), P(), P()),
        out_specs=(both,) * 4,
        check_vma=False,
    )
```

```python
import functools

import jax
import jax.numpy as jnp
import numpy as np
from jax import lax
from jax.experimental import pallas as pl
from jax.experimental.pallas import tpu as pltpu
from jax.sharding import Mesh
from jax.sharding import PartitionSpec as P

HEAD = 128
R_CAP = 2
RLEN = 128
PLEN = 256
HALF = 128
CHIPS = 16
CORES = 2
PIECE = HALF // CHIPS
UNIT = 2 * PIECE
WIDTH = 5120
TENSOR = 8
COLS = WIDTH // TENSOR
GROUPS = 8
SCALE = HEAD ** (-0.5)
EXP2_SCALE = SCALE * float(np.log2(np.e))
EPS = 1e-06
f32 = jnp.float32
bf16 = jnp.bfloat16
DP = ("x_hi", "z", "core")
SPREAD = ("x_hi", "z")
X_LO = 2
Y = 4
PROJECT_VMEM = 60 << 20
SMEM = pl.BlockSpec(memory_space=pltpu.SMEM)


def rope_tables():
    freqs = 1000000.0 ** (-np.arange(HEAD // 2, dtype=np.float64) * 2.0 / HEAD)
    angles = np.arange(PLEN, dtype=np.float64)[:, None] * freqs[None, :]
    cos, sin = np.cos(angles), np.sin(angles)
    shape = (CORES, HALF, HEAD)
    c = np.concatenate([cos, cos], axis=1).astype(np.float32).reshape(shape)
    s = np.concatenate([-sin, sin], axis=1).astype(np.float32).reshape(shape)
    return c, s


def swap_halves(u):
    return pltpu.roll(u, HEAD // 2, 1)


def to_units(keys, values):
    n = keys.shape[0] // PIECE
    return jnp.concatenate(
        [keys.reshape(n, PIECE, HEAD), values.reshape(n, PIECE, HEAD)], axis=1
    )


def from_units(units):
    u = units.astype(f32)
    n = u.shape[0]
    return u[:, :PIECE].reshape(n * PIECE, HEAD), u[:, PIECE:].reshape(n * PIECE, HEAD)


def dot_nn(a, b):
    return lax.dot_general(a, b, (((1,), (0,)), ((), ())), preferred_element_type=f32)


def dot_nt(a, b):
    return lax.dot_general(a, b, (((1,), (1,)), ((), ())), preferred_element_type=f32)


def project_kernel(
    x_ref, wk_ref, wv_ref, gain_ref, c_ref, s_ref, units_ref, *refs
):
    send_refs, (x_s, w_s, c_s, s_s, sems, table_sems, send_sems) = refs[:Y - 1], refs[Y - 1:]
    core, y = lax.axis_index("core"), lax.axis_index("y")
    order = [(k, half) for k in range(1, Y) for half in range(X_LO)] + [(0, 0), (0, 1)]
    copies = []
    for n, (k, half) in enumerate(order):
        rows = pl.ds(pl.multiple_of((half * Y + (y ^ k)) * COLS, COLS), COLS)
        copies.append(
            [
                pltpu.make_async_copy(wk_ref.at[rows], w_s.at[n, 0], sems.at[n, 1]),
                pltpu.make_async_copy(wv_ref.at[rows], w_s.at[n, 1], sems.at[n, 2]),
                pltpu.make_async_copy(x_ref.at[:, rows], x_s.at[n], sems.at[n, 0]),
            ]
        )
        for copy in copies[-1]:
            copy.start()
    tables = [
        pltpu.make_async_copy(c_ref.at[core], c_s, table_sems.at[0]),
        pltpu.make_async_copy(s_ref.at[core], s_s, table_sems.at[1]),
    ]
    for copy in tables:
        copy.start()
    sends = [
        pltpu.make_async_copy(w_s.at[n], send_refs[k - 1].at[half], send_sems.at[n])
        for n, (k, half) in enumerate(order)
        if k
    ]
    acc = jnp.zeros((HALF, 2 * HEAD), f32)
    for n in range(TENSOR):
        for copy in copies[n]:
            copy.wait()
        if n < len(sends):
            sends[n].start()
        acc += dot_nn(x_s[n], jnp.concatenate([w_s[n, 0], w_s[n, 1]], axis=1))
    for copy in tables:
        copy.wait()
    raw = acc[:, :HEAD]
    inv = lax.rsqrt(jnp.mean(raw * raw, axis=-1, keepdims=True) + EPS)
    u = raw * inv * gain_ref[...]
    keys = u * c_s[...] + swap_halves(u) * s_s[...]
    high = raw.astype(bf16).astype(f32)
    parts = [keys, acc[:, HEAD:], high, raw - high]
    units_ref[...] = jnp.concatenate(
        [part.reshape(CHIPS, PIECE, HEAD) for part in parts], axis=1
    ).astype(bf16)
    for copy in sends:
        copy.wait()


def project(x, wk, wv, gain, c, s):
    vmem = pl.BlockSpec(memory_space=pltpu.VMEM)
    hbm = pl.BlockSpec(memory_space=pltpu.HBM)
    anywhere = pl.BlockSpec(memory_space=pl.ANY)
    return pl.pallas_call(
        project_kernel,
        in_specs=[hbm, hbm, hbm, vmem, hbm, hbm],
        out_specs=[vmem] + [anywhere] * (Y - 1),
        out_shape=[jax.ShapeDtypeStruct((CHIPS, 2 * UNIT, HEAD), bf16)]
        + [jax.ShapeDtypeStruct((X_LO, 2, COLS, HEAD), bf16)] * (Y - 1),
        scratch_shapes=[
            pltpu.VMEM((TENSOR, HALF, COLS), bf16),
            pltpu.VMEM((TENSOR, 2, COLS, HEAD), bf16),
            pltpu.VMEM((HALF, HEAD), f32),
            pltpu.VMEM((HALF, HEAD), f32),
            pltpu.SemaphoreType.DMA((TENSOR, 3)),
            pltpu.SemaphoreType.DMA((2,)),
            pltpu.SemaphoreType.DMA((TENSOR - X_LO,)),
        ],
        compiler_params=pltpu.CompilerParams(vmem_limit_bytes=PROJECT_VMEM),
        cost_estimate=pl.CostEstimate(flops=2 * HALF * WIDTH * 256, bytes_accessed=4 << 20, transcendentals=0),
        name="project",
    )(x, wk, wv, gain, c, s)


def select_kernel(slot_prompt_ref, owner_ref, mine_ref, other_ref, out_ref):
    core = lax.axis_index("core")
    for chip in range(CHIPS):
        for r in range(R_CAP):
            q = owner_ref[slot_prompt_ref[chip * CORES * R_CAP + core * R_CAP + r]]
            out_ref[chip, r, 0] = mine_ref[q, :UNIT]
            out_ref[chip, r, 1] = other_ref[q, :UNIT]


def select(slot_prompt, owner, mine, other):
    vmem = pl.BlockSpec(memory_space=pltpu.VMEM)
    return pl.pallas_call(
        select_kernel,
        in_specs=[SMEM, SMEM, vmem, vmem],
        out_specs=vmem,
        out_shape=jax.ShapeDtypeStruct((CHIPS, R_CAP, 2, UNIT, HEAD), bf16),
        compiler_params=pltpu.CompilerParams(vmem_limit_bytes=8 << 20),
        name="select",
    )(slot_prompt, owner, mine, other)


def attend_kernel(
    counts_ref, slot_prompt_ref, lengths_ref,
    kv_ref, q_ref, g_ref, rk_ref, rv_ref,
    dq_ref, drk_ref, drv_ref, grads_ref,
    ds_s, pb_s,
):
    slot = pl.program_id(0)
    core, dp = lax.axis_index("core"), lax.axis_index(DP)
    live = slot < counts_ref[dp]

    @pl.when(live)
    def _():
        length = lengths_ref[slot_prompt_ref[dp * R_CAP + slot]]
        ka, va = from_units(kv_ref[:, 0, 0])
        kb, vb = from_units(kv_ref[:, 0, 1])
        keys = jnp.concatenate([ka.astype(bf16), kb.astype(bf16), rk_ref[...]], axis=0)
        values = jnp.concatenate([va.astype(bf16), vb.astype(bf16), rv_ref[...]], axis=0)
        row = lax.broadcasted_iota(jnp.int32, (HALF, RLEN), 0)
        query = lax.broadcasted_iota(jnp.int32, (HALF, RLEN), 1)
        seen = jnp.concatenate(
            [
                row + core * HALF < length,
                row + (1 - core) * HALF < length,
                row <= query,
            ],
            axis=0,
        )
        for h in range(GROUPS):
            cols = slice(h * HEAD, (h + 1) * HEAD)
            qh = q_ref[:, cols]
            gh = g_ref[:, cols]
            st = jnp.where(seen, dot_nt(keys, qh), -jnp.inf)
            dpt = dot_nt(values, gh)
            top = jnp.max(st, axis=0, keepdims=True)
            e = jnp.exp2((st - top) * EXP2_SCALE)
            inv = 1.0 / jnp.sum(e, axis=0, keepdims=True)
            p = e * inv
            pb = p.astype(bf16)
            pb_s[:, cols] = pb
            delta = jnp.sum(pb.astype(f32) * dpt, axis=0, keepdims=True)
            ds_s[:, cols] = (p * ((dpt - delta) * SCALE)).astype(bf16)
        q_rows = jnp.concatenate([q_ref[:, h * HEAD:(h + 1) * HEAD] for h in range(GROUPS)], axis=0)
        g_rows = jnp.concatenate([g_ref[:, h * HEAD:(h + 1) * HEAD] for h in range(GROUPS)], axis=0)
        dk = dot_nn(ds_s[...], q_rows)
        dv = dot_nn(pb_s[...], g_rows)
        grads_ref[:, 0, 0] = to_units(dk[:HALF], dv[:HALF]).astype(bf16)
        grads_ref[:, 0, 1] = to_units(dk[HALF:PLEN], dv[HALF:PLEN]).astype(bf16)
        drk_ref[...] = dk[PLEN:].astype(bf16)
        drv_ref[...] = dv[PLEN:].astype(bf16)
        keys_t = keys.T
        for h in range(GROUPS):
            cols = slice(h * HEAD, (h + 1) * HEAD)
            dq_ref[:, cols] = dot_nn(keys_t, ds_s[:, cols]).T.astype(bf16)

    @pl.when(jnp.logical_not(live))
    def _():
        grads_ref[...] = jnp.zeros_like(grads_ref)
        drk_ref[...] = jnp.zeros_like(drk_ref)
        drv_ref[...] = jnp.zeros_like(drv_ref)
        dq_ref[...] = jnp.zeros_like(dq_ref)


def attend(counts, slot_prompt, lengths, kv, q, g, rk, rv):
    width = GROUPS * HEAD
    rows = lambda n: pl.BlockSpec((RLEN, n), lambda i: (i, 0))
    units = pl.BlockSpec((CHIPS, 1, 2, UNIT, HEAD), lambda i: (0, i, 0, 0, 0))
    return pl.pallas_call(
        attend_kernel,
        grid=(R_CAP,),
        in_specs=[SMEM] * 3 + [units, rows(width), rows(width), rows(HEAD), rows(HEAD)],
        out_specs=[rows(width), rows(HEAD), rows(HEAD), units],
        out_shape=[
            jax.ShapeDtypeStruct((R_CAP * RLEN, width), bf16),
            jax.ShapeDtypeStruct((R_CAP * RLEN, HEAD), bf16),
            jax.ShapeDtypeStruct((R_CAP * RLEN, HEAD), bf16),
            jax.ShapeDtypeStruct((CHIPS, R_CAP, 2, UNIT, HEAD), bf16),
        ],
        scratch_shapes=[
            pltpu.VMEM((PLEN + RLEN, width), bf16),
            pltpu.VMEM((PLEN + RLEN, width), bf16),
        ],
        compiler_params=pltpu.CompilerParams(vmem_limit_bytes=24 << 20),
        cost_estimate=pl.CostEstimate(flops=10 * 2 * 384 * 1024 * 128, bytes_accessed=3 << 20, transcendentals=2 * 384 * 1024),
        name="attend",
    )(counts, slot_prompt, lengths, kv, q, g, rk, rv)


def collect_kernel(slot_prompt_ref, owner_ref, got_ref, mine_ref, other_ref, acc):
    core = lax.axis_index("core")
    acc[...] = jnp.zeros_like(acc)
    for chip in range(CHIPS):
        for r in range(R_CAP):
            q = owner_ref[slot_prompt_ref[chip * CORES * R_CAP + core * R_CAP + r]]
            acc[q] += got_ref[chip, r].astype(f32)
    mine_ref[...] = acc[:, 0]
    other_ref[...] = acc[:, 1].astype(bf16)


def collect(slot_prompt, owner, got):
    vmem = pl.BlockSpec(memory_space=pltpu.VMEM)
    return pl.pallas_call(
        collect_kernel,
        in_specs=[SMEM, SMEM, vmem],
        out_specs=[vmem, vmem],
        out_shape=[
            jax.ShapeDtypeStruct((CHIPS, UNIT, HEAD), f32),
            jax.ShapeDtypeStruct((CHIPS, UNIT, HEAD), bf16),
        ],
        scratch_shapes=[pltpu.VMEM((CHIPS, 2, UNIT, HEAD), f32)],
        compiler_params=pltpu.CompilerParams(vmem_limit_bytes=8 << 20),
        name="collect",
    )(slot_prompt, owner, got)


def unkey_kernel(sum_ref, other_ref, units_ref, gain_ref, c_ref, s_ref, out_ref):
    core, chip = lax.axis_index("core"), lax.axis_index(SPREAD)
    rows = pl.ds(pl.multiple_of(chip * PIECE, PIECE), PIECE)
    cos, sin = c_ref[core, rows], s_ref[core, rows]
    total = sum_ref[...] + other_ref[...].astype(f32)
    units = units_ref[...].astype(f32)
    dk, dv = total[:, :PIECE], total[:, PIECE:]
    raw = units[:, UNIT:UNIT + PIECE] + units[:, UNIT + PIECE:]
    inv = lax.rsqrt(jnp.mean(raw * raw, axis=-1, keepdims=True) + EPS)
    turned = swap_halves((dk * sin).reshape(HALF, HEAD)).reshape(CHIPS, PIECE, HEAD)
    dn = (dk * cos + turned) * gain_ref[...]
    dot = jnp.mean(raw * dn, axis=-1, keepdims=True)
    d_raw = inv * (dn - raw * (inv * inv * dot))
    out_ref[...] = jnp.concatenate(
        [d_raw.reshape(HALF, HEAD), dv.reshape(HALF, HEAD)], axis=1
    ).astype(bf16)


def unkey(sums, other, units, gain, c, s):
    vmem = pl.BlockSpec(memory_space=pltpu.VMEM)
    return pl.pallas_call(
        unkey_kernel,
        in_specs=[vmem] * 6,
        out_specs=vmem,
        out_shape=jax.ShapeDtypeStruct((HALF, 2 * HEAD), bf16),
        compiler_params=pltpu.CompilerParams(vmem_limit_bytes=8 << 20),
        name="unkey",
    )(sums, other, units, gain, c, s)


def input_grad_kernel(wk_ref, wv_ref, *refs):
    grads, got, (out_ref, w_s, sems) = refs[:Y], refs[Y:2 * Y - 1], refs[2 * Y - 1:]
    y = lax.axis_index("y")
    order = [(k, half) for half in range(X_LO) for k in range(Y)]
    copies = []
    for n, (k, half) in enumerate(order):
        if k:
            copies.append([pltpu.make_async_copy(got[k - 1].at[half], w_s.at[n], sems.at[n, 0])])
        else:
            rows = pl.ds(pl.multiple_of((half * Y + y) * COLS, COLS), COLS)
            copies.append(
                [
                    pltpu.make_async_copy(w.at[rows], w_s.at[n, j], sems.at[n, j])
                    for j, w in enumerate((wk_ref, wv_ref))
                ]
            )
        for copy in copies[-1]:
            copy.start()
    for half in range(X_LO):
        total = jnp.zeros((HALF, COLS), f32)
        for k in range(Y):
            n = half * Y + k
            for copy in copies[n]:
                copy.wait()
            total += dot_nt(grads[k][...], jnp.concatenate([w_s[n, 0], w_s[n, 1]], axis=1))
        out_ref[:, half] = total.reshape(CHIPS, PIECE, COLS).astype(bf16)


def input_grad(wk, wv, grads, got):
    vmem = pl.BlockSpec(memory_space=pltpu.VMEM)
    hbm = pl.BlockSpec(memory_space=pltpu.HBM)
    return pl.pallas_call(
        input_grad_kernel,
        in_specs=[hbm, hbm] + [vmem] * Y + [hbm] * (Y - 1),
        out_specs=vmem,
        out_shape=jax.ShapeDtypeStruct((CHIPS, X_LO, PIECE, COLS), bf16),
        scratch_shapes=[
            pltpu.VMEM((TENSOR, 2, COLS, HEAD), bf16),
            pltpu.SemaphoreType.DMA((TENSOR, 2)),
        ],
        compiler_params=pltpu.CompilerParams(vmem_limit_bytes=PROJECT_VMEM),
        cost_estimate=pl.CostEstimate(flops=2 * HALF * WIDTH * 256, bytes_accessed=4 << 20, transcendentals=0),
        name="input_grad",
    )(wk, wv, *grads, *got)


def together(first, second):
    flat, tree = jax.tree.flatten((first, second))
    return jax.tree.unflatten(tree, lax.optimization_barrier(flat))


def swap_y(x, k):
    return lax.ppermute(x, "y", [(i, i ^ k) for i in range(Y)])


def spread(x):
    return lax.all_to_all(x, SPREAD, 0, 0, tiled=True)


def swap_cores(x):
    return lax.ppermute(x, "core", [(0, 1), (1, 0)])


def on_device(
    prompt_x, key_matrix, value_matrix, k_gain, queries, response_keys, response_values,
    output_gradient, response_counts, slot_prompt, prompt_owner, prompt_lengths,
):
    c, s = rope_tables()
    gain = k_gain.reshape(1, HEAD)
    with jax.named_scope("keys_out"):
        units, *send = project(prompt_x, key_matrix, value_matrix, gain, c, s)
        got = [swap_y(send[k - 1], k) for k in range(1, Y)]
        mine = spread(units)
        needed = select(slot_prompt, prompt_owner, mine, swap_cores(mine))
        needed, got[0] = together(needed, got[0])
        needed, got[2] = together(spread(needed), got[2])
    with jax.named_scope("attention"):
        dq, drk, drv, grads = attend(
            response_counts, slot_prompt, prompt_lengths,
            needed, queries, output_gradient, response_keys, response_values,
        )
    with jax.named_scope("grads_back"):
        sums, other = collect(slot_prompt, prompt_owner, spread(grads))
        other, got[1] = together(other, got[1])
        both = unkey(sums, swap_cores(other), mine, gain, c, s)
        both = [both] + [swap_y(both, k) for k in range(1, Y)]
    with jax.named_scope("input_grad"):
        shares = input_grad(key_matrix, value_matrix, both, got)
        shares = shares.reshape(CHIPS * X_LO, PIECE, COLS)
        shares = lax.all_to_all(shares, SPREAD + ("x_lo",), 0, 0, tiled=True)
        shares = shares.reshape(CHIPS, X_LO, PIECE, COLS).astype(f32)
        d_prompt = jnp.sum(shares, axis=1).reshape(HALF, COLS).astype(bf16)
    return dq, drk, drv, d_prompt


def solution(mesh):
    fine = Mesh(mesh.devices.reshape(2, 8, 2, 2, 4), ("x_hi", "z", "core", "x_lo", "y"))
    dp, tensor = ("x_hi", "z", "core"), ("x_lo", "y")
    both = P(dp, tensor)
    return jax.shard_map(
        on_device,
        mesh=fine,
        in_specs=(P(dp, None), P(None, tensor), P(None, tensor), P(), both, both, both, both, P(), P(), P(), P()),
        out_specs=(both,) * 4,
        check_vma=False,
    )
```

```python
import functools

import jax
import jax.numpy as jnp
import numpy as np
from jax import lax
from jax.experimental import pallas as pl
from jax.experimental.pallas import tpu as pltpu
from jax.sharding import Mesh
from jax.sharding import PartitionSpec as P

HEAD = 128
R_CAP = 2
RLEN = 128
PLEN = 256
HALF = 128
CHIPS = 16
CORES = 2
PIECE = HALF // CHIPS
UNIT = 2 * PIECE
WIDTH = 5120
TENSOR = 8
COLS = WIDTH // TENSOR
GROUPS = 8
SCALE = HEAD ** (-0.5)
EXP2_SCALE = SCALE * float(np.log2(np.e))
EPS = 1e-06
FAR = -1e30
PAIRS = 2
DQ = True
f32 = jnp.float32
bf16 = jnp.bfloat16
DP = ("x_hi", "z", "core")
SPREAD = ("x_hi", "z")
X_LO = 2
Y = 4
PROJECT_VMEM = 60 << 20
SMEM = pl.BlockSpec(memory_space=pltpu.SMEM)


def rope_table():
    freqs = 1000000.0 ** (-np.arange(HEAD // 2, dtype=np.float64) * 2.0 / HEAD)
    angles = np.arange(PLEN, dtype=np.float64)[:, None] * freqs[None, :]
    both = np.concatenate([np.cos(angles), np.sin(angles)], axis=1)
    return both.astype(np.float32).reshape(CORES, HALF, HEAD)


def cos_sin(table):
    first = lax.broadcasted_iota(jnp.int32, table.shape, 1) < HEAD // 2
    turned = swap_halves(table)
    return jnp.where(first, table, turned), jnp.where(first, -turned, table)


def swap_halves(u):
    return pltpu.roll(u, HEAD // 2, 1)


def to_units(keys, values):
    n = keys.shape[0] // PIECE
    return jnp.concatenate(
        [keys.reshape(n, PIECE, HEAD), values.reshape(n, PIECE, HEAD)], axis=1
    )


def from_units(units):
    u = units.astype(f32)
    n = u.shape[0]
    return u[:, :PIECE].reshape(n * PIECE, HEAD), u[:, PIECE:].reshape(n * PIECE, HEAD)


def dot_nn(a, b):
    return lax.dot_general(a, b, (((1,), (0,)), ((), ())), preferred_element_type=f32)


def dot_nt(a, b):
    return lax.dot_general(a, b, (((1,), (1,)), ((), ())), preferred_element_type=f32)


def project_kernel(
    x_ref, wk_ref, wv_ref, gain_ref, table_ref, units_ref, *refs
):
    send_refs, (x_s, w_s, table_s, sems, table_sem, send_sems) = refs[:Y - 1], refs[Y - 1:]
    core, y = lax.axis_index("core"), lax.axis_index("y")
    order = [(k, half) for k in range(1, Y) for half in range(X_LO)] + [(0, 0), (0, 1)]
    copies = []
    for n, (k, half) in enumerate(order):
        rows = pl.ds(pl.multiple_of((half * Y + (y ^ k)) * COLS, COLS), COLS)
        copies.append(
            [
                pltpu.make_async_copy(wk_ref.at[rows], w_s.at[n, 0], sems.at[n, 1]),
                pltpu.make_async_copy(wv_ref.at[rows], w_s.at[n, 1], sems.at[n, 2]),
                pltpu.make_async_copy(x_ref.at[:, rows], x_s.at[n], sems.at[n, 0]),
            ]
        )
        for copy in copies[-1]:
            copy.start()
    table = pltpu.make_async_copy(table_ref.at[core], table_s, table_sem)
    table.start()
    sends = [
        pltpu.make_async_copy(w_s.at[n], send_refs[k - 1].at[half], send_sems.at[n])
        for n, (k, half) in enumerate(order)
        if k
    ]
    acc = jnp.zeros((HALF, 2 * HEAD), f32)
    for n in range(TENSOR):
        for copy in copies[n]:
            copy.wait()
        if n < len(sends):
            sends[n].start()
        acc += dot_nn(x_s[n], jnp.concatenate([w_s[n, 0], w_s[n, 1]], axis=1))
    table.wait()
    cos, sin = cos_sin(table_s[...])
    raw = acc[:, :HEAD]
    inv = lax.rsqrt(jnp.mean(raw * raw, axis=-1, keepdims=True) + EPS)
    u = raw * inv * gain_ref[...]
    keys = u * cos + swap_halves(u) * sin
    high = raw.astype(bf16).astype(f32)
    parts = [keys, acc[:, HEAD:], high, raw - high]
    units_ref[...] = jnp.concatenate(
        [part.reshape(CHIPS, PIECE, HEAD) for part in parts], axis=1
    ).astype(bf16)
    for copy in sends:
        copy.wait()


def project(x, wk, wv, gain, table):
    vmem = pl.BlockSpec(memory_space=pltpu.VMEM)
    hbm = pl.BlockSpec(memory_space=pltpu.HBM)
    anywhere = pl.BlockSpec(memory_space=pl.ANY)
    return pl.pallas_call(
        project_kernel,
        in_specs=[hbm, hbm, hbm, vmem, hbm],
        out_specs=[vmem] + [anywhere] * (Y - 1),
        out_shape=[jax.ShapeDtypeStruct((CHIPS, 2 * UNIT, HEAD), bf16)]
        + [jax.ShapeDtypeStruct((X_LO, 2, COLS, HEAD), bf16)] * (Y - 1),
        scratch_shapes=[
            pltpu.VMEM((TENSOR, HALF, COLS), bf16),
            pltpu.VMEM((TENSOR, 2, COLS, HEAD), bf16),
            pltpu.VMEM((HALF, HEAD), f32),
            pltpu.SemaphoreType.DMA((TENSOR, 3)),
            pltpu.SemaphoreType.DMA(()),
            pltpu.SemaphoreType.DMA((TENSOR - X_LO,)),
        ],
        compiler_params=pltpu.CompilerParams(vmem_limit_bytes=PROJECT_VMEM),
        cost_estimate=pl.CostEstimate(flops=2 * HALF * WIDTH * 256, bytes_accessed=4 << 20, transcendentals=0),
        name="project",
    )(x, wk, wv, gain, table)


def select_kernel(slot_prompt_ref, owner_ref, mine_ref, other_ref, out_ref):
    core = lax.axis_index("core")
    for chip in range(CHIPS):
        for r in range(R_CAP):
            q = owner_ref[slot_prompt_ref[chip * CORES * R_CAP + core * R_CAP + r]]
            out_ref[chip, r, 0] = mine_ref[q, :UNIT]
            out_ref[chip, r, 1] = other_ref[q, :UNIT]


def select(slot_prompt, owner, mine, other):
    vmem = pl.BlockSpec(memory_space=pltpu.VMEM)
    return pl.pallas_call(
        select_kernel,
        in_specs=[SMEM, SMEM, vmem, vmem],
        out_specs=vmem,
        out_shape=jax.ShapeDtypeStruct((CHIPS, R_CAP, 2, UNIT, HEAD), bf16),
        compiler_params=pltpu.CompilerParams(vmem_limit_bytes=8 << 20),
        name="select",
    )(slot_prompt, owner, mine, other)


def attend_slot(core, length, pairs, kv_ref, q_ref, g_ref, rk_ref, rv_ref, dq_ref, drk_ref, drv_ref, grads_ref, ds_s, pb_s):
    ka, va = from_units(kv_ref[:, 0])
    kb, vb = from_units(kv_ref[:, 1])
    keys = jnp.concatenate([ka.astype(bf16), kb.astype(bf16), rk_ref[...]], axis=0)
    values = jnp.concatenate([va.astype(bf16), vb.astype(bf16), rv_ref[...]], axis=0)
    row = lax.broadcasted_iota(jnp.int32, (HALF, HEAD), 0)
    column = lax.broadcasted_iota(jnp.int32, (HALF, HEAD), 1)
    hidden = lambda first: jnp.where((column == 0) & (row + first >= length), FAR, 0.0)
    far = jnp.concatenate(
        [
            hidden(core * HALF),
            hidden((1 - core) * HALF),
            jnp.where((column == row) & (row > 0), FAR, 0.0),
        ],
        axis=0,
    ).astype(bf16)
    early = jnp.where((column == 0) | (column > row), 1.0, 0.0).astype(bf16)
    keys_far = jnp.concatenate([keys, far], axis=1)
    for h in range(0, GROUPS, pairs):
        cols = slice(h * HEAD, (h + pairs) * HEAD)
        stack = lambda ref: jnp.concatenate([ref[:, (h + i) * HEAD:(h + i + 1) * HEAD] for i in range(pairs)], axis=0)
        qh = jnp.concatenate([stack(q_ref), jnp.concatenate([early] * pairs, axis=0)], axis=1)
        st = dot_nt(keys_far, qh)
        dpt = dot_nt(values, stack(g_ref))
        top = jnp.max(st, axis=0, keepdims=True)
        e = jnp.exp2((st - top) * EXP2_SCALE)
        inv = 1.0 / jnp.sum(e, axis=0, keepdims=True)
        delta = jnp.sum(e * dpt, axis=0, keepdims=True) * inv
        p = e * inv
        pb_s[:, cols] = p.astype(bf16)
        ds_s[:, cols] = (p * (dpt - delta)).astype(bf16)
    rows_of = lambda ref: jnp.concatenate([ref[:, h * HEAD:(h + 1) * HEAD] for h in range(GROUPS)], axis=0)
    dk = dot_nn(ds_s[...], rows_of(q_ref)) * SCALE
    dv = dot_nn(pb_s[...], rows_of(g_ref))
    grads_ref[:, 0] = to_units(dk[:HALF], dv[:HALF]).astype(bf16)
    grads_ref[:, 1] = to_units(dk[HALF:PLEN], dv[HALF:PLEN]).astype(bf16)
    drk_ref[...] = dk[PLEN:].astype(bf16)
    drv_ref[...] = dv[PLEN:].astype(bf16)
    if DQ:
        keys_t = keys.T
        for h in range(GROUPS):
            cols = slice(h * HEAD, (h + 1) * HEAD)
            dq_ref[:, cols] = (dot_nn(keys_t, ds_s[:, cols]) * SCALE).T.astype(bf16)


def attend_kernel(
    counts_ref, slot_prompt_ref, lengths_ref,
    kv_ref, q_ref, g_ref, rk_ref, rv_ref,
    dq_ref, drk_ref, drv_ref, grads_ref,
    ds_s, pb_s,
):
    core, dp = lax.axis_index("core"), lax.axis_index(DP)
    for slot in range(R_CAP):
        rows = pl.ds(slot * RLEN, RLEN)
        kv = kv_ref.at[:, slot]
        ins = [r.at[rows] for r in (q_ref, g_ref, rk_ref, rv_ref)]
        outs = [r.at[rows] for r in (dq_ref, drk_ref, drv_ref)] + [grads_ref.at[:, slot]]

        def run():
            length = lengths_ref[slot_prompt_ref[dp * R_CAP + slot]]
            attend_slot(core, length, PAIRS, kv, *ins, *outs, ds_s, pb_s)

        def clear():
            for out in outs:
                out[...] = jnp.zeros(out.shape, out.dtype)

        live = slot < counts_ref[dp]
        pl.when(live)(run)
        pl.when(jnp.logical_not(live))(clear)


def attend(counts, slot_prompt, lengths, kv, q, g, rk, rv):
    width = GROUPS * HEAD
    vmem = pl.BlockSpec(memory_space=pltpu.VMEM)
    return pl.pallas_call(
        attend_kernel,
        in_specs=[SMEM] * 3 + [vmem] * 5,
        out_specs=[vmem] * 4,
        out_shape=[
            jax.ShapeDtypeStruct((R_CAP * RLEN, width), bf16),
            jax.ShapeDtypeStruct((R_CAP * RLEN, HEAD), bf16),
            jax.ShapeDtypeStruct((R_CAP * RLEN, HEAD), bf16),
            jax.ShapeDtypeStruct((CHIPS, R_CAP, 2, UNIT, HEAD), bf16),
        ],
        scratch_shapes=[
            pltpu.VMEM((PLEN + RLEN, width), bf16),
            pltpu.VMEM((PLEN + RLEN, width), bf16),
        ],
        compiler_params=pltpu.CompilerParams(vmem_limit_bytes=16 << 20),
        cost_estimate=pl.CostEstimate(flops=10 * 2 * 384 * 1024 * 128, bytes_accessed=3 << 20, transcendentals=2 * 384 * 1024),
        name="attend",
    )(counts, slot_prompt, lengths, kv, q, g, rk, rv)


def collect_kernel(slot_prompt_ref, owner_ref, got_ref, mine_ref, other_ref, acc):
    core = lax.axis_index("core")
    acc[...] = jnp.zeros_like(acc)
    for chip in range(CHIPS):
        for r in range(R_CAP):
            q = owner_ref[slot_prompt_ref[chip * CORES * R_CAP + core * R_CAP + r]]
            acc[q] += got_ref[chip, r].astype(f32)
    mine_ref[...] = acc[:, 0]
    other_ref[...] = acc[:, 1].astype(bf16)


def collect(slot_prompt, owner, got):
    vmem = pl.BlockSpec(memory_space=pltpu.VMEM)
    return pl.pallas_call(
        collect_kernel,
        in_specs=[SMEM, SMEM, vmem],
        out_specs=[vmem, vmem],
        out_shape=[
            jax.ShapeDtypeStruct((CHIPS, UNIT, HEAD), f32),
            jax.ShapeDtypeStruct((CHIPS, UNIT, HEAD), bf16),
        ],
        scratch_shapes=[pltpu.VMEM((CHIPS, 2, UNIT, HEAD), f32)],
        compiler_params=pltpu.CompilerParams(vmem_limit_bytes=8 << 20),
        name="collect",
    )(slot_prompt, owner, got)


def unkey_kernel(sum_ref, other_ref, units_ref, gain_ref, table_ref, out_ref):
    core, chip = lax.axis_index("core"), lax.axis_index(SPREAD)
    rows = pl.ds(pl.multiple_of(chip * PIECE, PIECE), PIECE)
    cos, sin = cos_sin(table_ref[core, rows])
    total = sum_ref[...] + other_ref[...].astype(f32)
    units = units_ref[...].astype(f32)
    dk, dv = total[:, :PIECE], total[:, PIECE:]
    raw = units[:, UNIT:UNIT + PIECE] + units[:, UNIT + PIECE:]
    inv = lax.rsqrt(jnp.mean(raw * raw, axis=-1, keepdims=True) + EPS)
    turned = swap_halves((dk * sin).reshape(HALF, HEAD)).reshape(CHIPS, PIECE, HEAD)
    dn = (dk * cos + turned) * gain_ref[...]
    dot = jnp.mean(raw * dn, axis=-1, keepdims=True)
    d_raw = inv * (dn - raw * (inv * inv * dot))
    out_ref[...] = jnp.concatenate(
        [d_raw.reshape(HALF, HEAD), dv.reshape(HALF, HEAD)], axis=1
    ).astype(bf16)


def unkey(sums, other, units, gain, table):
    vmem = pl.BlockSpec(memory_space=pltpu.VMEM)
    return pl.pallas_call(
        unkey_kernel,
        in_specs=[vmem] * 5,
        out_specs=vmem,
        out_shape=jax.ShapeDtypeStruct((HALF, 2 * HEAD), bf16),
        compiler_params=pltpu.CompilerParams(vmem_limit_bytes=8 << 20),
        name="unkey",
    )(sums, other, units, gain, table)


def input_grad_kernel(wk_ref, wv_ref, *refs):
    grads, got, out_ref = refs[:Y], refs[Y:2 * Y - 1], refs[-1]
    y = lax.axis_index("y")
    for half in range(X_LO):
        rows = pl.ds(pl.multiple_of((half * Y + y) * COLS, COLS), COLS)
        total = dot_nt(grads[0][...], jnp.concatenate([wk_ref[rows], wv_ref[rows]], axis=1))
        for k in range(1, Y):
            w = jnp.concatenate([got[k - 1][half, 0], got[k - 1][half, 1]], axis=1)
            total += dot_nt(grads[k][...], w)
        out_ref[:, half] = total.reshape(CHIPS, PIECE, COLS).astype(bf16)


def input_grad(wk, wv, grads, got):
    vmem = pl.BlockSpec(memory_space=pltpu.VMEM)
    return pl.pallas_call(
        input_grad_kernel,
        in_specs=[vmem] * (2 * Y + 1),
        out_specs=vmem,
        out_shape=jax.ShapeDtypeStruct((CHIPS, X_LO, PIECE, COLS), bf16),
        compiler_params=pltpu.CompilerParams(vmem_limit_bytes=16 << 20),
        cost_estimate=pl.CostEstimate(flops=2 * HALF * WIDTH * 256, bytes_accessed=4 << 20, transcendentals=0),
        name="input_grad",
    )(wk, wv, *grads, *got)


def together(first, second):
    flat, tree = jax.tree.flatten((first, second))
    return jax.tree.unflatten(tree, lax.optimization_barrier(flat))


def swap_y(x, k):
    return lax.ppermute(x, "y", [(i, i ^ k) for i in range(Y)])


def spread(x):
    return lax.all_to_all(x, SPREAD, 0, 0, tiled=True)


def swap_cores(x):
    return lax.ppermute(x, "core", [(0, 1), (1, 0)])


def on_device(
    prompt_x, key_matrix, value_matrix, k_gain, queries, response_keys, response_values,
    output_gradient, response_counts, slot_prompt, prompt_owner, prompt_lengths,
):
    table = rope_table()
    gain = k_gain.reshape(1, HEAD)
    with jax.named_scope("keys_out"):
        units, *send = project(prompt_x, key_matrix, value_matrix, gain, table)
        got = [swap_y(send[k - 1], k) for k in (1, 3)]
        mine = spread(units)
        needed = select(slot_prompt, prompt_owner, mine, swap_cores(mine))
        needed, got = together(needed, got)
        needed = spread(needed)
    with jax.named_scope("attention"):
        dq, drk, drv, grads = attend(
            response_counts, slot_prompt, prompt_lengths,
            needed, queries, output_gradient, response_keys, response_values,
        )
    with jax.named_scope("grads_back"):
        grads, late = together(grads, send[1])
        got.insert(1, swap_y(late, 2))
        sums, other = collect(slot_prompt, prompt_owner, spread(grads))
        both = unkey(sums, swap_cores(other), mine, gain, table)
        both = [both] + [swap_y(both, k) for k in range(1, Y)]
    with jax.named_scope("input_grad"):
        shares = input_grad(key_matrix, value_matrix, both, got)
        shares = shares.reshape(CHIPS * X_LO, PIECE, COLS)
        shares = lax.all_to_all(shares, SPREAD + ("x_lo",), 0, 0, tiled=True)
        shares = shares.reshape(CHIPS, X_LO, PIECE, COLS).astype(f32)
        d_prompt = jnp.sum(shares, axis=1).reshape(HALF, COLS).astype(bf16)
    return dq, drk, drv, d_prompt


def solution(mesh):
    fine = Mesh(mesh.devices.reshape(2, 8, 2, 2, 4), ("x_hi", "z", "core", "x_lo", "y"))
    dp, tensor = ("x_hi", "z", "core"), ("x_lo", "y")
    both = P(dp, tensor)
    return jax.shard_map(
        on_device,
        mesh=fine,
        in_specs=(P(dp, None), P(None, tensor), P(None, tensor), P(), both, both, both, both, P(), P(), P(), P()),
        out_specs=(both,) * 4,
        check_vma=False,
    )
```

```python
import functools

import jax
import jax.numpy as jnp
import numpy as np
from jax import lax
from jax.experimental import pallas as pl
from jax.experimental.pallas import tpu as pltpu
from jax.sharding import Mesh
from jax.sharding import PartitionSpec as P

HEAD = 128
R_CAP = 2
RLEN = 128
PLEN = 256
HALF = 128
CHIPS = 16
CORES = 2
PIECE = HALF // CHIPS
UNIT = 2 * PIECE
WIDTH = 5120
TENSOR = 8
COLS = WIDTH // TENSOR
GROUPS = 8
SCALE = HEAD ** (-0.5)
EXP2_SCALE = SCALE * float(np.log2(np.e))
EPS = 1e-06
FAR = -1e30
PAIRS = 4
f32 = jnp.float32
bf16 = jnp.bfloat16
DP = ("x_hi", "z", "core")
SPREAD = ("x_hi", "z")
X_LO = 2
Y = 4
PROJECT_VMEM = 60 << 20
SMEM = pl.BlockSpec(memory_space=pltpu.SMEM)


def rope_table():
    freqs = 1000000.0 ** (-np.arange(HEAD // 2, dtype=np.float64) * 2.0 / HEAD)
    angles = np.arange(PLEN, dtype=np.float64)[:, None] * freqs[None, :]
    both = np.concatenate([np.cos(angles), np.sin(angles)], axis=1)
    return both.astype(np.float32).reshape(CORES, HALF, HEAD)


def cos_sin(table):
    first = lax.broadcasted_iota(jnp.int32, table.shape, 1) < HEAD // 2
    turned = swap_halves(table)
    return jnp.where(first, table, turned), jnp.where(first, -turned, table)


def swap_halves(u):
    return pltpu.roll(u, HEAD // 2, 1)


def to_units(keys, values):
    n = keys.shape[0] // PIECE
    return jnp.concatenate(
        [keys.reshape(n, PIECE, HEAD), values.reshape(n, PIECE, HEAD)], axis=1
    )


def from_units(units):
    u = units.astype(f32)
    n = u.shape[0]
    return u[:, :PIECE].reshape(n * PIECE, HEAD), u[:, PIECE:].reshape(n * PIECE, HEAD)


def dot_nn(a, b):
    return lax.dot_general(a, b, (((1,), (0,)), ((), ())), preferred_element_type=f32)


def dot_nt(a, b):
    return lax.dot_general(a, b, (((1,), (1,)), ((), ())), preferred_element_type=f32)


def project_kernel(
    x_ref, wk_ref, wv_ref, gain_ref, table_ref, units_ref, *refs
):
    send_refs, (x_s, w_s, table_s, sems, table_sem, send_sems) = refs[:Y - 1], refs[Y - 1:]
    core, y = lax.axis_index("core"), lax.axis_index("y")
    order = [(k, half) for k in range(1, Y) for half in range(X_LO)] + [(0, 0), (0, 1)]
    copies = []
    for n, (k, half) in enumerate(order):
        rows = pl.ds(pl.multiple_of((half * Y + (y ^ k)) * COLS, COLS), COLS)
        copies.append(
            [
                pltpu.make_async_copy(wk_ref.at[rows], w_s.at[n, 0], sems.at[n, 1]),
                pltpu.make_async_copy(wv_ref.at[rows], w_s.at[n, 1], sems.at[n, 2]),
                pltpu.make_async_copy(x_ref.at[:, rows], x_s.at[n], sems.at[n, 0]),
            ]
        )
        for copy in copies[-1]:
            copy.start()
    table = pltpu.make_async_copy(table_ref.at[core], table_s, table_sem)
    table.start()
    sends = [
        pltpu.make_async_copy(w_s.at[n], send_refs[k - 1].at[half], send_sems.at[n])
        for n, (k, half) in enumerate(order)
        if k
    ]
    acc = jnp.zeros((HALF, 2 * HEAD), f32)
    for n in range(TENSOR):
        for copy in copies[n]:
            copy.wait()
        if n < len(sends):
            sends[n].start()
        acc += dot_nn(x_s[n], jnp.concatenate([w_s[n, 0], w_s[n, 1]], axis=1))
    table.wait()
    cos, sin = cos_sin(table_s[...])
    raw = acc[:, :HEAD]
    inv = lax.rsqrt(jnp.mean(raw * raw, axis=-1, keepdims=True) + EPS)
    u = raw * inv * gain_ref[...]
    keys = u * cos + swap_halves(u) * sin
    high = raw.astype(bf16).astype(f32)
    parts = [keys, acc[:, HEAD:], high, raw - high]
    units_ref[...] = jnp.concatenate(
        [part.reshape(CHIPS, PIECE, HEAD) for part in parts], axis=1
    ).astype(bf16)
    for copy in sends:
        copy.wait()


def project(x, wk, wv, gain, table):
    vmem = pl.BlockSpec(memory_space=pltpu.VMEM)
    hbm = pl.BlockSpec(memory_space=pltpu.HBM)
    anywhere = pl.BlockSpec(memory_space=pl.ANY)
    return pl.pallas_call(
        project_kernel,
        in_specs=[hbm, hbm, hbm, vmem, hbm],
        out_specs=[vmem] + [anywhere] * (Y - 1),
        out_shape=[jax.ShapeDtypeStruct((CHIPS, 2 * UNIT, HEAD), bf16)]
        + [jax.ShapeDtypeStruct((X_LO, 2, COLS, HEAD), bf16)] * (Y - 1),
        scratch_shapes=[
            pltpu.VMEM((TENSOR, HALF, COLS), bf16),
            pltpu.VMEM((TENSOR, 2, COLS, HEAD), bf16),
            pltpu.VMEM((HALF, HEAD), f32),
            pltpu.SemaphoreType.DMA((TENSOR, 3)),
            pltpu.SemaphoreType.DMA(()),
            pltpu.SemaphoreType.DMA((TENSOR - X_LO,)),
        ],
        compiler_params=pltpu.CompilerParams(vmem_limit_bytes=PROJECT_VMEM),
        cost_estimate=pl.CostEstimate(flops=2 * HALF * WIDTH * 256, bytes_accessed=4 << 20, transcendentals=0),
        name="project",
    )(x, wk, wv, gain, table)


def select_kernel(slot_prompt_ref, owner_ref, mine_ref, other_ref, out_ref):
    core = lax.axis_index("core")
    for chip in range(CHIPS):
        for r in range(R_CAP):
            q = owner_ref[slot_prompt_ref[chip * CORES * R_CAP + core * R_CAP + r]]
            out_ref[chip, r, 0] = mine_ref[q, :UNIT]
            out_ref[chip, r, 1] = other_ref[q, :UNIT]


def select(slot_prompt, owner, mine, other):
    vmem = pl.BlockSpec(memory_space=pltpu.VMEM)
    return pl.pallas_call(
        select_kernel,
        in_specs=[SMEM, SMEM, vmem, vmem],
        out_specs=vmem,
        out_shape=jax.ShapeDtypeStruct((CHIPS, R_CAP, 2, UNIT, HEAD), bf16),
        compiler_params=pltpu.CompilerParams(vmem_limit_bytes=8 << 20),
        name="select",
    )(slot_prompt, owner, mine, other)


def attend_slot(core, length, live, kv_ref, q_ref, g_ref, rk_ref, rv_ref, dq_ref, drk_ref, drv_ref, grads_ref, ds_s, pb_s):
    ka, va = from_units(kv_ref[:, 0])
    kb, vb = from_units(kv_ref[:, 1])
    keys = jnp.concatenate([ka.astype(bf16), kb.astype(bf16), rk_ref[...]], axis=0)
    values = jnp.concatenate([va.astype(bf16), vb.astype(bf16), rv_ref[...]], axis=0)
    row = lax.broadcasted_iota(jnp.int32, (HALF, HEAD), 0)
    column = lax.broadcasted_iota(jnp.int32, (HALF, HEAD), 1)
    hidden = lambda first: jnp.where((column == 0) & (row + first >= length), FAR, 0.0)
    far = jnp.concatenate(
        [
            hidden(core * HALF),
            hidden((1 - core) * HALF),
            jnp.where((column == row) & (row > 0), FAR, 0.0),
        ],
        axis=0,
    ).astype(bf16)
    early = jnp.where((column == 0) | (column > row), 1.0, 0.0).astype(bf16)
    keys_far = jnp.concatenate([keys, far], axis=1)
    for h in range(0, GROUPS, PAIRS):
        cols = slice(h * HEAD, (h + PAIRS) * HEAD)
        stack = lambda ref: jnp.concatenate([ref[:, (h + i) * HEAD:(h + i + 1) * HEAD] for i in range(PAIRS)], axis=0)
        qh = jnp.concatenate([stack(q_ref), jnp.concatenate([early] * PAIRS, axis=0)], axis=1)
        st = dot_nt(keys_far, qh)
        dpt = dot_nt(values, stack(g_ref))
        top = jnp.max(st, axis=0, keepdims=True)
        e = jnp.exp2((st - top) * EXP2_SCALE)
        inv = 1.0 / jnp.sum(e, axis=0, keepdims=True)
        delta = jnp.sum(e * dpt, axis=0, keepdims=True) * inv
        p = e * inv
        pb_s[:, cols] = p.astype(bf16)
        ds_s[:, cols] = (p * (dpt - delta)).astype(bf16)
    rows_of = lambda ref: jnp.concatenate([ref[:, h * HEAD:(h + 1) * HEAD] for h in range(GROUPS)], axis=0)
    keep = jnp.where(live, 1.0, 0.0)
    kept = lambda x: x * keep
    dk = kept(dot_nn(ds_s[...], rows_of(q_ref)) * SCALE)
    dv = kept(dot_nn(pb_s[...], rows_of(g_ref)))
    grads_ref[:, 0] = to_units(dk[:HALF], dv[:HALF]).astype(bf16)
    grads_ref[:, 1] = to_units(dk[HALF:PLEN], dv[HALF:PLEN]).astype(bf16)
    drk_ref[...] = dk[PLEN:].astype(bf16)
    drv_ref[...] = dv[PLEN:].astype(bf16)
    keys_t = keys.T
    for h in range(GROUPS):
        cols = slice(h * HEAD, (h + 1) * HEAD)
        dq_ref[:, cols] = kept((dot_nn(keys_t, ds_s[:, cols]) * SCALE).T).astype(bf16)


def entry(ref, index):
    row = ref[...]
    here = lax.broadcasted_iota(jnp.int32, row.shape, 1) == index
    return jnp.sum(jnp.where(here, row, 0).astype(f32), axis=1, keepdims=True).astype(jnp.int32)


def attend_kernel(
    counts_ref, slot_prompt_ref, lengths_ref,
    kv_ref, q_ref, g_ref, rk_ref, rv_ref,
    dq_ref, drk_ref, drv_ref, grads_ref,
    ds_s, pb_s,
):
    core, dp = lax.axis_index("core"), lax.axis_index(DP)
    for slot in range(R_CAP):
        rows = pl.ds(slot * RLEN, RLEN)
        kv = kv_ref.at[:, slot]
        ins = [r.at[rows] for r in (q_ref, g_ref, rk_ref, rv_ref)]
        outs = [r.at[rows] for r in (dq_ref, drk_ref, drv_ref)] + [grads_ref.at[:, slot]]

        prompt = entry(slot_prompt_ref, dp * R_CAP + slot)
        length = entry(lengths_ref, prompt)
        live = entry(counts_ref, dp) > slot
        attend_slot(core, length, live, kv, *ins, *outs, ds_s.at[slot], pb_s.at[slot])


def attend(counts, slot_prompt, lengths, kv, q, g, rk, rv):
    width = GROUPS * HEAD
    vmem = pl.BlockSpec(memory_space=pltpu.VMEM)
    return pl.pallas_call(
        attend_kernel,
        in_specs=[vmem] * 8,
        out_specs=[vmem] * 4,
        out_shape=[
            jax.ShapeDtypeStruct((R_CAP * RLEN, width), bf16),
            jax.ShapeDtypeStruct((R_CAP * RLEN, HEAD), bf16),
            jax.ShapeDtypeStruct((R_CAP * RLEN, HEAD), bf16),
            jax.ShapeDtypeStruct((CHIPS, R_CAP, 2, UNIT, HEAD), bf16),
        ],
        scratch_shapes=[
            pltpu.VMEM((R_CAP, PLEN + RLEN, width), bf16),
            pltpu.VMEM((R_CAP, PLEN + RLEN, width), bf16),
        ],
        compiler_params=pltpu.CompilerParams(vmem_limit_bytes=16 << 20),
        cost_estimate=pl.CostEstimate(flops=10 * 2 * 384 * 1024 * 128, bytes_accessed=3 << 20, transcendentals=2 * 384 * 1024),
        name="attend",
    )(counts.reshape(1, -1), slot_prompt.reshape(1, -1), lengths.reshape(1, -1), kv, q, g, rk, rv)


def collect_kernel(slot_prompt_ref, owner_ref, got_ref, mine_ref, other_ref, acc):
    core = lax.axis_index("core")
    acc[...] = jnp.zeros_like(acc)
    for chip in range(CHIPS):
        for r in range(R_CAP):
            q = owner_ref[slot_prompt_ref[chip * CORES * R_CAP + core * R_CAP + r]]
            acc[q] += got_ref[chip, r].astype(f32)
    mine_ref[...] = acc[:, 0]
    other_ref[...] = acc[:, 1].astype(bf16)


def collect(slot_prompt, owner, got):
    vmem = pl.BlockSpec(memory_space=pltpu.VMEM)
    return pl.pallas_call(
        collect_kernel,
        in_specs=[SMEM, SMEM, vmem],
        out_specs=[vmem, vmem],
        out_shape=[
            jax.ShapeDtypeStruct((CHIPS, UNIT, HEAD), f32),
            jax.ShapeDtypeStruct((CHIPS, UNIT, HEAD), bf16),
        ],
        scratch_shapes=[pltpu.VMEM((CHIPS, 2, UNIT, HEAD), f32)],
        compiler_params=pltpu.CompilerParams(vmem_limit_bytes=8 << 20),
        name="collect",
    )(slot_prompt, owner, got)


def unkey_kernel(sum_ref, other_ref, units_ref, gain_ref, table_ref, out_ref):
    core, chip = lax.axis_index("core"), lax.axis_index(SPREAD)
    rows = pl.ds(pl.multiple_of(chip * PIECE, PIECE), PIECE)
    cos, sin = cos_sin(table_ref[core, rows])
    total = sum_ref[...] + other_ref[...].astype(f32)
    units = units_ref[...].astype(f32)
    dk, dv = total[:, :PIECE], total[:, PIECE:]
    raw = units[:, UNIT:UNIT + PIECE] + units[:, UNIT + PIECE:]
    inv = lax.rsqrt(jnp.mean(raw * raw, axis=-1, keepdims=True) + EPS)
    turned = swap_halves((dk * sin).reshape(HALF, HEAD)).reshape(CHIPS, PIECE, HEAD)
    dn = (dk * cos + turned) * gain_ref[...]
    dot = jnp.mean(raw * dn, axis=-1, keepdims=True)
    d_raw = inv * (dn - raw * (inv * inv * dot))
    out_ref[...] = jnp.concatenate(
        [d_raw.reshape(HALF, HEAD), dv.reshape(HALF, HEAD)], axis=1
    ).astype(bf16)


def unkey(sums, other, units, gain, table):
    vmem = pl.BlockSpec(memory_space=pltpu.VMEM)
    return pl.pallas_call(
        unkey_kernel,
        in_specs=[vmem] * 5,
        out_specs=vmem,
        out_shape=jax.ShapeDtypeStruct((HALF, 2 * HEAD), bf16),
        compiler_params=pltpu.CompilerParams(vmem_limit_bytes=8 << 20),
        name="unkey",
    )(sums, other, units, gain, table)


def input_grad_kernel(wk_ref, wv_ref, *refs):
    grads, got, out_ref = refs[:Y], refs[Y:2 * Y - 1], refs[-1]
    y = lax.axis_index("y")
    for half in range(X_LO):
        rows = pl.ds(pl.multiple_of((half * Y + y) * COLS, COLS), COLS)
        total = dot_nt(grads[0][...], jnp.concatenate([wk_ref[rows], wv_ref[rows]], axis=1))
        for k in range(1, Y):
            w = jnp.concatenate([got[k - 1][half, 0], got[k - 1][half, 1]], axis=1)
            total += dot_nt(grads[k][...], w)
        out_ref[:, half] = total.reshape(CHIPS, PIECE, COLS).astype(bf16)


def input_grad(wk, wv, grads, got):
    vmem = pl.BlockSpec(memory_space=pltpu.VMEM)
    return pl.pallas_call(
        input_grad_kernel,
        in_specs=[vmem] * (2 * Y + 1),
        out_specs=vmem,
        out_shape=jax.ShapeDtypeStruct((CHIPS, X_LO, PIECE, COLS), bf16),
        compiler_params=pltpu.CompilerParams(vmem_limit_bytes=16 << 20),
        cost_estimate=pl.CostEstimate(flops=2 * HALF * WIDTH * 256, bytes_accessed=4 << 20, transcendentals=0),
        name="input_grad",
    )(wk, wv, *grads, *got)


def together(first, second):
    flat, tree = jax.tree.flatten((first, second))
    return jax.tree.unflatten(tree, lax.optimization_barrier(flat))


def swap_y(x, k):
    return lax.ppermute(x, "y", [(i, i ^ k) for i in range(Y)])


def spread(x):
    return lax.all_to_all(x, SPREAD, 0, 0, tiled=True)


def swap_cores(x):
    return lax.ppermute(x, "core", [(0, 1), (1, 0)])


def on_device(
    prompt_x, key_matrix, value_matrix, k_gain, queries, response_keys, response_values,
    output_gradient, response_counts, slot_prompt, prompt_owner, prompt_lengths,
):
    table = rope_table()
    gain = k_gain.reshape(1, HEAD)
    with jax.named_scope("keys_out"):
        units, *send = project(prompt_x, key_matrix, value_matrix, gain, table)
        got = [swap_y(send[k - 1], k) for k in range(1, Y)]
        mine = spread(units)
        needed = select(slot_prompt, prompt_owner, mine, swap_cores(mine))
        needed, (got[0], got[2]) = together(spread(needed), (got[0], got[2]))
    with jax.named_scope("attention"):
        dq, drk, drv, grads = attend(
            response_counts, slot_prompt, prompt_lengths,
            needed, queries, output_gradient, response_keys, response_values,
        )
    with jax.named_scope("grads_back"):
        sums, other = collect(slot_prompt, prompt_owner, spread(grads))
        other, got[1] = together(other, got[1])
        both = unkey(sums, swap_cores(other), mine, gain, table)
        both = [both] + [swap_y(both, k) for k in range(1, Y)]
    with jax.named_scope("input_grad"):
        shares = input_grad(key_matrix, value_matrix, both, got)
        shares = shares.reshape(CHIPS * X_LO, PIECE, COLS)
        shares = lax.all_to_all(shares, SPREAD + ("x_lo",), 0, 0, tiled=True)
        shares = shares.reshape(CHIPS, X_LO, PIECE, COLS).astype(f32)
        d_prompt = jnp.sum(shares, axis=1).reshape(HALF, COLS).astype(bf16)
    return dq, drk, drv, d_prompt


def solution(mesh):
    fine = Mesh(mesh.devices.reshape(2, 8, 2, 2, 4), ("x_hi", "z", "core", "x_lo", "y"))
    dp, tensor = ("x_hi", "z", "core"), ("x_lo", "y")
    both = P(dp, tensor)
    return jax.shard_map(
        on_device,
        mesh=fine,
        in_specs=(P(dp, None), P(None, tensor), P(None, tensor), P(), both, both, both, both, P(), P(), P(), P()),
        out_specs=(both,) * 4,
        check_vma=False,
    )
```

```python
import functools

import jax
import jax.numpy as jnp
import numpy as np
from jax import lax
from jax.experimental import pallas as pl
from jax.experimental.pallas import tpu as pltpu
from jax.sharding import Mesh
from jax.sharding import PartitionSpec as P

HEAD = 128
R_CAP = 2
RLEN = 128
PLEN = 256
HALF = 128
CHIPS = 16
CORES = 2
PIECE = HALF // CHIPS
UNIT = 2 * PIECE
WIDTH = 5120
TENSOR = 8
COLS = WIDTH // TENSOR
GROUPS = 8
SCALE = HEAD ** (-0.5)
EXP2_SCALE = SCALE * float(np.log2(np.e))
EPS = 1e-06
FAR = -1e30
PAIRS = 4
f32 = jnp.float32
bf16 = jnp.bfloat16
DP = ("x_hi", "z", "core")
SPREAD = ("x_hi", "z")
X_LO = 2
Y = 4
PROJECT_VMEM = 60 << 20
SMEM = pl.BlockSpec(memory_space=pltpu.SMEM)


def rope_table():
    freqs = 1000000.0 ** (-np.arange(HEAD // 2, dtype=np.float64) * 2.0 / HEAD)
    angles = np.arange(PLEN, dtype=np.float64)[:, None] * freqs[None, :]
    both = np.concatenate([np.cos(angles), np.sin(angles)], axis=1)
    return both.astype(np.float32).reshape(CORES, HALF, HEAD)


def cos_sin(table):
    first = lax.broadcasted_iota(jnp.int32, table.shape, 1) < HEAD // 2
    turned = swap_halves(table)
    return jnp.where(first, table, turned), jnp.where(first, -turned, table)


def swap_halves(u):
    return pltpu.roll(u, HEAD // 2, 1)


def to_units(keys, values):
    n = keys.shape[0] // PIECE
    return jnp.concatenate(
        [keys.reshape(n, PIECE, HEAD), values.reshape(n, PIECE, HEAD)], axis=1
    )


def from_units(units):
    u = units.astype(f32)
    n = u.shape[0]
    return u[:, :PIECE].reshape(n * PIECE, HEAD), u[:, PIECE:].reshape(n * PIECE, HEAD)


def dot_nn(a, b):
    return lax.dot_general(a, b, (((1,), (0,)), ((), ())), preferred_element_type=f32)


def dot_nt(a, b):
    return lax.dot_general(a, b, (((1,), (1,)), ((), ())), preferred_element_type=f32)


def project_kernel(
    x_ref, wk_ref, wv_ref, gain_ref, table_ref, units_ref, *refs
):
    send_refs, (x_s, w_s, table_s, gain_s, sems, small_sems, send_sems) = refs[:Y - 1], refs[Y - 1:]
    core, y = lax.axis_index("core"), lax.axis_index("y")
    order = [(k, half) for k in range(1, Y) for half in range(X_LO)] + [(0, 0), (0, 1)]
    copies = []
    for n, (k, half) in enumerate(order):
        rows = pl.ds(pl.multiple_of((half * Y + (y ^ k)) * COLS, COLS), COLS)
        copies.append(
            [
                pltpu.make_async_copy(wk_ref.at[rows], w_s.at[n, 0], sems.at[n, 1]),
                pltpu.make_async_copy(wv_ref.at[rows], w_s.at[n, 1], sems.at[n, 2]),
                pltpu.make_async_copy(x_ref.at[:, rows], x_s.at[n], sems.at[n, 0]),
            ]
        )
        for copy in copies[-1]:
            copy.start()
    small = [
        pltpu.make_async_copy(table_ref.at[core], table_s, small_sems.at[0]),
        pltpu.make_async_copy(gain_ref, gain_s, small_sems.at[1]),
    ]
    for copy in small:
        copy.start()
    sends = [
        pltpu.make_async_copy(w_s.at[n], send_refs[k - 1].at[half], send_sems.at[n])
        for n, (k, half) in enumerate(order)
        if k
    ]
    acc = jnp.zeros((HALF, 2 * HEAD), f32)
    for n in range(TENSOR):
        for copy in copies[n]:
            copy.wait()
        if n < len(sends):
            sends[n].start()
        acc += dot_nn(x_s[n], jnp.concatenate([w_s[n, 0], w_s[n, 1]], axis=1))
    for copy in small:
        copy.wait()
    cos, sin = cos_sin(table_s[...])
    raw = acc[:, :HEAD]
    inv = lax.rsqrt(jnp.mean(raw * raw, axis=-1, keepdims=True) + EPS)
    u = raw * inv * gain_s[...]
    keys = u * cos + swap_halves(u) * sin
    high = raw.astype(bf16).astype(f32)
    parts = [keys, acc[:, HEAD:], high, raw - high]
    units_ref[...] = jnp.concatenate(
        [part.reshape(CHIPS, PIECE, HEAD) for part in parts], axis=1
    ).astype(bf16)
    for copy in sends:
        copy.wait()


def project(x, wk, wv, gain, table):
    vmem = pl.BlockSpec(memory_space=pltpu.VMEM)
    hbm = pl.BlockSpec(memory_space=pltpu.HBM)
    anywhere = pl.BlockSpec(memory_space=pl.ANY)
    return pl.pallas_call(
        project_kernel,
        in_specs=[hbm] * 5,
        out_specs=[vmem] + [anywhere] * (Y - 1),
        out_shape=[jax.ShapeDtypeStruct((CHIPS, 2 * UNIT, HEAD), bf16)]
        + [jax.ShapeDtypeStruct((X_LO, 2, COLS, HEAD), bf16)] * (Y - 1),
        scratch_shapes=[
            pltpu.VMEM((TENSOR, HALF, COLS), bf16),
            pltpu.VMEM((TENSOR, 2, COLS, HEAD), bf16),
            pltpu.VMEM((HALF, HEAD), f32),
            pltpu.VMEM((1, HEAD), f32),
            pltpu.SemaphoreType.DMA((TENSOR, 3)),
            pltpu.SemaphoreType.DMA((2,)),
            pltpu.SemaphoreType.DMA((TENSOR - X_LO,)),
        ],
        compiler_params=pltpu.CompilerParams(vmem_limit_bytes=PROJECT_VMEM),
        cost_estimate=pl.CostEstimate(flops=2 * HALF * WIDTH * 256, bytes_accessed=4 << 20, transcendentals=0),
        name="project",
    )(x, wk, wv, gain, table)


def select_kernel(slot_prompt_ref, owner_ref, mine_ref, other_ref, out_ref):
    core = lax.axis_index("core")
    for chip in range(CHIPS):
        for r in range(R_CAP):
            q = owner_ref[slot_prompt_ref[chip * CORES * R_CAP + core * R_CAP + r]]
            out_ref[chip, r, 0] = mine_ref[q, :UNIT]
            out_ref[chip, r, 1] = other_ref[q, :UNIT]


def select(slot_prompt, owner, mine, other):
    vmem = pl.BlockSpec(memory_space=pltpu.VMEM)
    return pl.pallas_call(
        select_kernel,
        in_specs=[SMEM, SMEM, vmem, vmem],
        out_specs=vmem,
        out_shape=jax.ShapeDtypeStruct((CHIPS, R_CAP, 2, UNIT, HEAD), bf16),
        compiler_params=pltpu.CompilerParams(vmem_limit_bytes=8 << 20),
        name="select",
    )(slot_prompt, owner, mine, other)


def attend_slot(core, length, live, kv_ref, q_ref, g_ref, rk_ref, rv_ref, dq_ref, drk_ref, drv_ref, grads_ref, ds_s, pb_s):
    ka, va = from_units(kv_ref[:, 0])
    kb, vb = from_units(kv_ref[:, 1])
    keys = jnp.concatenate([ka.astype(bf16), kb.astype(bf16), rk_ref[...]], axis=0)
    values = jnp.concatenate([va.astype(bf16), vb.astype(bf16), rv_ref[...]], axis=0)
    row = lax.broadcasted_iota(jnp.int32, (HALF, HEAD), 0)
    column = lax.broadcasted_iota(jnp.int32, (HALF, HEAD), 1)
    hidden = lambda first: jnp.where((column == 0) & (row + first >= length), FAR, 0.0)
    far = jnp.concatenate(
        [
            hidden(core * HALF),
            hidden((1 - core) * HALF),
            jnp.where((column == row) & (row > 0), FAR, 0.0),
        ],
        axis=0,
    ).astype(bf16)
    early = jnp.where((column == 0) | (column > row), 1.0, 0.0).astype(bf16)
    keys_far = jnp.concatenate([keys, far], axis=1)
    for h in range(0, GROUPS, PAIRS):
        cols = slice(h * HEAD, (h + PAIRS) * HEAD)
        stack = lambda ref: jnp.concatenate([ref[:, (h + i) * HEAD:(h + i + 1) * HEAD] for i in range(PAIRS)], axis=0)
        qh = jnp.concatenate([stack(q_ref), jnp.concatenate([early] * PAIRS, axis=0)], axis=1)
        st = dot_nt(keys_far, qh)
        dpt = dot_nt(values, stack(g_ref))
        top = jnp.max(st, axis=0, keepdims=True)
        e = jnp.exp2((st - top) * EXP2_SCALE)
        inv = 1.0 / jnp.sum(e, axis=0, keepdims=True)
        delta = jnp.sum(e * dpt, axis=0, keepdims=True) * inv
        p = e * inv
        pb_s[:, cols] = p.astype(bf16)
        ds_s[:, cols] = (p * (dpt - delta)).astype(bf16)
    rows_of = lambda ref: jnp.concatenate([ref[:, h * HEAD:(h + 1) * HEAD] for h in range(GROUPS)], axis=0)
    keep = jnp.where(live, 1.0, 0.0)
    kept = lambda x: x * keep
    dk = kept(dot_nn(ds_s[...], rows_of(q_ref)) * SCALE)
    dv = kept(dot_nn(pb_s[...], rows_of(g_ref)))
    grads_ref[:, 0] = to_units(dk[:HALF], dv[:HALF]).astype(bf16)
    grads_ref[:, 1] = to_units(dk[HALF:PLEN], dv[HALF:PLEN]).astype(bf16)
    drk_ref[...] = dk[PLEN:].astype(bf16)
    drv_ref[...] = dv[PLEN:].astype(bf16)
    keys_t = keys.T
    for h in range(GROUPS):
        cols = slice(h * HEAD, (h + 1) * HEAD)
        dq_ref[:, cols] = kept((dot_nn(keys_t, ds_s[:, cols]) * SCALE).T).astype(bf16)


def entry(ref, index):
    row = ref[...]
    here = lax.broadcasted_iota(jnp.int32, row.shape, 1) == index
    return jnp.sum(jnp.where(here, row, 0).astype(f32), axis=1, keepdims=True).astype(jnp.int32)


def attend_kernel(
    counts_ref, slot_prompt_ref, lengths_ref,
    kv_ref, q_ref, g_ref, rk_ref, rv_ref,
    dq_ref, drk_ref, drv_ref, grads_ref,
    ds_s, pb_s,
):
    core, dp = lax.axis_index("core"), lax.axis_index(DP)
    for slot in range(R_CAP):
        rows = pl.ds(slot * RLEN, RLEN)
        kv = kv_ref.at[:, slot]
        ins = [r.at[rows] for r in (q_ref, g_ref, rk_ref, rv_ref)]
        outs = [r.at[rows] for r in (dq_ref, drk_ref, drv_ref)] + [grads_ref.at[:, slot]]

        prompt = entry(slot_prompt_ref, dp * R_CAP + slot)
        length = entry(lengths_ref, prompt)
        live = entry(counts_ref, dp) > slot
        attend_slot(core, length, live, kv, *ins, *outs, ds_s.at[slot], pb_s.at[slot])


def attend(counts, slot_prompt, lengths, kv, q, g, rk, rv):
    width = GROUPS * HEAD
    vmem = pl.BlockSpec(memory_space=pltpu.VMEM)
    return pl.pallas_call(
        attend_kernel,
        in_specs=[vmem] * 8,
        out_specs=[vmem] * 4,
        out_shape=[
            jax.ShapeDtypeStruct((R_CAP * RLEN, width), bf16),
            jax.ShapeDtypeStruct((R_CAP * RLEN, HEAD), bf16),
            jax.ShapeDtypeStruct((R_CAP * RLEN, HEAD), bf16),
            jax.ShapeDtypeStruct((CHIPS, R_CAP, 2, UNIT, HEAD), bf16),
        ],
        scratch_shapes=[
            pltpu.VMEM((R_CAP, PLEN + RLEN, width), bf16),
            pltpu.VMEM((R_CAP, PLEN + RLEN, width), bf16),
        ],
        compiler_params=pltpu.CompilerParams(vmem_limit_bytes=16 << 20),
        cost_estimate=pl.CostEstimate(flops=10 * 2 * 384 * 1024 * 128, bytes_accessed=3 << 20, transcendentals=2 * 384 * 1024),
        name="attend",
    )(counts.reshape(1, -1), slot_prompt.reshape(1, -1), lengths.reshape(1, -1), kv, q, g, rk, rv)


def collect_kernel(slot_prompt_ref, owner_ref, got_ref, mine_ref, other_ref, acc):
    core = lax.axis_index("core")
    acc[...] = jnp.zeros_like(acc)
    for chip in range(CHIPS):
        for r in range(R_CAP):
            q = owner_ref[slot_prompt_ref[chip * CORES * R_CAP + core * R_CAP + r]]
            acc[q] += got_ref[chip, r].astype(f32)
    mine_ref[...] = acc[:, 0]
    other_ref[...] = acc[:, 1].astype(bf16)


def collect(slot_prompt, owner, got):
    vmem = pl.BlockSpec(memory_space=pltpu.VMEM)
    return pl.pallas_call(
        collect_kernel,
        in_specs=[SMEM, SMEM, vmem],
        out_specs=[vmem, vmem],
        out_shape=[
            jax.ShapeDtypeStruct((CHIPS, UNIT, HEAD), f32),
            jax.ShapeDtypeStruct((CHIPS, UNIT, HEAD), bf16),
        ],
        scratch_shapes=[pltpu.VMEM((CHIPS, 2, UNIT, HEAD), f32)],
        compiler_params=pltpu.CompilerParams(vmem_limit_bytes=8 << 20),
        name="collect",
    )(slot_prompt, owner, got)


def unkey_kernel(sum_ref, other_ref, units_ref, gain_ref, table_ref, out_ref):
    core, chip = lax.axis_index("core"), lax.axis_index(SPREAD)
    rows = pl.ds(pl.multiple_of(chip * PIECE, PIECE), PIECE)
    cos, sin = cos_sin(table_ref[core, rows])
    total = sum_ref[...] + other_ref[...].astype(f32)
    units = units_ref[...].astype(f32)
    dk, dv = total[:, :PIECE], total[:, PIECE:]
    raw = units[:, UNIT:UNIT + PIECE] + units[:, UNIT + PIECE:]
    inv = lax.rsqrt(jnp.mean(raw * raw, axis=-1, keepdims=True) + EPS)
    turned = swap_halves((dk * sin).reshape(HALF, HEAD)).reshape(CHIPS, PIECE, HEAD)
    dn = (dk * cos + turned) * gain_ref[...]
    dot = jnp.mean(raw * dn, axis=-1, keepdims=True)
    d_raw = inv * (dn - raw * (inv * inv * dot))
    out_ref[...] = jnp.concatenate(
        [d_raw.reshape(HALF, HEAD), dv.reshape(HALF, HEAD)], axis=1
    ).astype(bf16)


def unkey(sums, other, units, gain, table):
    vmem = pl.BlockSpec(memory_space=pltpu.VMEM)
    return pl.pallas_call(
        unkey_kernel,
        in_specs=[vmem] * 5,
        out_specs=vmem,
        out_shape=jax.ShapeDtypeStruct((HALF, 2 * HEAD), bf16),
        compiler_params=pltpu.CompilerParams(vmem_limit_bytes=8 << 20),
        name="unkey",
    )(sums, other, units, gain, table)


def input_grad_kernel(wk_ref, wv_ref, *refs):
    grads, got, out_ref = refs[:Y], refs[Y:2 * Y - 1], refs[-1]
    y = lax.axis_index("y")
    for half in range(X_LO):
        rows = pl.ds(pl.multiple_of((half * Y + y) * COLS, COLS), COLS)
        total = dot_nt(grads[0][...], jnp.concatenate([wk_ref[rows], wv_ref[rows]], axis=1))
        for k in range(1, Y):
            w = jnp.concatenate([got[k - 1][half, 0], got[k - 1][half, 1]], axis=1)
            total += dot_nt(grads[k][...], w)
        out_ref[:, half] = total.reshape(CHIPS, PIECE, COLS).astype(bf16)


def input_grad(wk, wv, grads, got):
    vmem = pl.BlockSpec(memory_space=pltpu.VMEM)
    return pl.pallas_call(
        input_grad_kernel,
        in_specs=[vmem] * (2 * Y + 1),
        out_specs=vmem,
        out_shape=jax.ShapeDtypeStruct((CHIPS, X_LO, PIECE, COLS), bf16),
        compiler_params=pltpu.CompilerParams(vmem_limit_bytes=16 << 20),
        cost_estimate=pl.CostEstimate(flops=2 * HALF * WIDTH * 256, bytes_accessed=4 << 20, transcendentals=0),
        name="input_grad",
    )(wk, wv, *grads, *got)


def together(first, second):
    flat, tree = jax.tree.flatten((first, second))
    return jax.tree.unflatten(tree, lax.optimization_barrier(flat))


def swap_y(x, k):
    return lax.ppermute(x, "y", [(i, i ^ k) for i in range(Y)])


def spread(x):
    return lax.all_to_all(x, SPREAD, 0, 0, tiled=True)


def swap_cores(x):
    return lax.ppermute(x, "core", [(0, 1), (1, 0)])


def on_device(
    prompt_x, key_matrix, value_matrix, k_gain, queries, response_keys, response_values,
    output_gradient, response_counts, slot_prompt, prompt_owner, prompt_lengths,
):
    table = rope_table()
    gain = k_gain.reshape(1, HEAD)
    with jax.named_scope("keys_out"):
        units, *send = project(prompt_x, key_matrix, value_matrix, gain, table)
        got = [swap_y(send[k - 1], k) for k in range(1, Y)]
        mine = spread(units)
        needed = select(slot_prompt, prompt_owner, mine, swap_cores(mine))
        needed, (got[0], got[2]) = together(spread(needed), (got[0], got[2]))
    with jax.named_scope("attention"):
        dq, drk, drv, grads = attend(
            response_counts, slot_prompt, prompt_lengths,
            needed, queries, output_gradient, response_keys, response_values,
        )
    with jax.named_scope("grads_back"):
        sums, other = collect(slot_prompt, prompt_owner, spread(grads))
        other, got[1] = together(other, got[1])
        both = unkey(sums, swap_cores(other), mine, gain, table)
        both = [both] + [swap_y(both, k) for k in range(1, Y)]
    with jax.named_scope("input_grad"):
        shares = input_grad(key_matrix, value_matrix, both, got)
        shares = shares.reshape(CHIPS * X_LO, PIECE, COLS)
        shares = lax.all_to_all(shares, SPREAD + ("x_lo",), 0, 0, tiled=True)
        shares = shares.reshape(CHIPS, X_LO, PIECE, COLS).astype(f32)
        d_prompt = jnp.sum(shares, axis=1).reshape(HALF, COLS).astype(bf16)
    return dq, drk, drv, d_prompt


def solution(mesh):
    fine = Mesh(mesh.devices.reshape(2, 8, 2, 2, 4), ("x_hi", "z", "core", "x_lo", "y"))
    dp, tensor = ("x_hi", "z", "core"), ("x_lo", "y")
    both = P(dp, tensor)
    return jax.shard_map(
        on_device,
        mesh=fine,
        in_specs=(P(dp, None), P(None, tensor), P(None, tensor), P(), both, both, both, both, P(), P(), P(), P()),
        out_specs=(both,) * 4,
        check_vma=False,
    )
```

```python
import functools

import jax
import jax.numpy as jnp
import numpy as np
from jax import lax
from jax.experimental import pallas as pl
from jax.experimental.pallas import tpu as pltpu
from jax.sharding import Mesh
from jax.sharding import PartitionSpec as P

HEAD = 128
R_CAP = 2
RLEN = 128
PLEN = 256
HALF = 128
CHIPS = 16
CORES = 2
PROMPTS = 16
PIECE = HALF // CHIPS
UNIT = 2 * PIECE
WIDTH = 5120
TENSOR = 8
COLS = WIDTH // TENSOR
GROUPS = 8
SCALE = HEAD ** (-0.5)
EXP2_SCALE = SCALE * float(np.log2(np.e))
EPS = 1e-06
FAR = -1e30
PAIRS = 2
f32 = jnp.float32
bf16 = jnp.bfloat16
DP = ("x_hi", "z", "core")
SPREAD = ("x_hi", "z")
X_LO = 2
Y = 4
PROJECT_VMEM = 60 << 20
LAST_FAR = (1, 3, 2)


def rope_table():
    freqs = 1000000.0 ** (-np.arange(HEAD // 2, dtype=np.float64) * 2.0 / HEAD)
    angles = np.arange(PLEN, dtype=np.float64)[:, None] * freqs[None, :]
    both = np.concatenate([np.cos(angles), np.sin(angles)], axis=1)
    return both.astype(np.float32).reshape(CORES, HALF, HEAD)


def cos_sin(table):
    first = lax.broadcasted_iota(jnp.int32, table.shape, 1) < HEAD // 2
    turned = swap_halves(table)
    return jnp.where(first, table, turned), jnp.where(first, -turned, table)


def swap_halves(u):
    return pltpu.roll(u, HEAD // 2, 1)


def to_units(keys, values):
    n = keys.shape[0] // PIECE
    return jnp.concatenate(
        [keys.reshape(n, PIECE, HEAD), values.reshape(n, PIECE, HEAD)], axis=1
    )


def from_units(units):
    u = units.astype(f32)
    n = u.shape[0]
    return u[:, :PIECE].reshape(n * PIECE, HEAD), u[:, PIECE:].reshape(n * PIECE, HEAD)


def dot_nn(a, b):
    return lax.dot_general(a, b, (((1,), (0,)), ((), ())), preferred_element_type=f32)


def dot_nt(a, b):
    return lax.dot_general(a, b, (((1,), (1,)), ((), ())), preferred_element_type=f32)


def project_kernel(
    x_ref, wk_ref, wv_ref, gain_ref, table_ref, units_ref, *refs
):
    send_refs, (x_s, w_s, table_s, gain_s, sems, small_sems, send_sems) = refs[:Y - 1], refs[Y - 1:]
    core, y = lax.axis_index("core"), lax.axis_index("y")
    order = [(k, half) for k in range(1, Y) for half in range(X_LO)] + [(0, 0), (0, 1)]
    copies = []
    for n, (k, half) in enumerate(order):
        rows = pl.ds(pl.multiple_of((half * Y + (y ^ k)) * COLS, COLS), COLS)
        copies.append(
            [
                pltpu.make_async_copy(wk_ref.at[rows], w_s.at[n, 0], sems.at[n, 1]),
                pltpu.make_async_copy(wv_ref.at[rows], w_s.at[n, 1], sems.at[n, 2]),
                pltpu.make_async_copy(x_ref.at[:, rows], x_s.at[n], sems.at[n, 0]),
            ]
        )
        for copy in copies[-1]:
            copy.start()
    small = [
        pltpu.make_async_copy(table_ref.at[core], table_s, small_sems.at[0]),
        pltpu.make_async_copy(gain_ref, gain_s, small_sems.at[1]),
    ]
    for copy in small:
        copy.start()
    sends = [
        pltpu.make_async_copy(w_s.at[n], send_refs[k - 1].at[half], send_sems.at[n])
        for n, (k, half) in enumerate(order)
        if k
    ]
    acc = jnp.zeros((HALF, 2 * HEAD), f32)
    for n in range(TENSOR):
        for copy in copies[n]:
            copy.wait()
        if n < len(sends):
            sends[n].start()
        acc += dot_nn(x_s[n], jnp.concatenate([w_s[n, 0], w_s[n, 1]], axis=1))
    for copy in small:
        copy.wait()
    cos, sin = cos_sin(table_s[...])
    raw = acc[:, :HEAD]
    inv = lax.rsqrt(jnp.mean(raw * raw, axis=-1, keepdims=True) + EPS)
    u = raw * inv * gain_s[...]
    keys = u * cos + swap_halves(u) * sin
    high = raw.astype(bf16).astype(f32)
    parts = [keys, acc[:, HEAD:], high, raw - high]
    units_ref[...] = jnp.concatenate(
        [part.reshape(CHIPS, PIECE, HEAD) for part in parts], axis=1
    ).astype(bf16)
    for copy in sends:
        copy.wait()


def project(x, wk, wv, gain, table):
    vmem = pl.BlockSpec(memory_space=pltpu.VMEM)
    hbm = pl.BlockSpec(memory_space=pltpu.HBM)
    anywhere = pl.BlockSpec(memory_space=pl.ANY)
    return pl.pallas_call(
        project_kernel,
        in_specs=[hbm] * 5,
        out_specs=[vmem] + [anywhere] * (Y - 1),
        out_shape=[jax.ShapeDtypeStruct((CHIPS, 2 * UNIT, HEAD), bf16)]
        + [jax.ShapeDtypeStruct((X_LO, 2, COLS, HEAD), bf16)] * (Y - 1),
        scratch_shapes=[
            pltpu.VMEM((TENSOR, HALF, COLS), bf16),
            pltpu.VMEM((TENSOR, 2, COLS, HEAD), bf16),
            pltpu.VMEM((HALF, HEAD), f32),
            pltpu.VMEM((1, HEAD), f32),
            pltpu.SemaphoreType.DMA((TENSOR, 3)),
            pltpu.SemaphoreType.DMA((2,)),
            pltpu.SemaphoreType.DMA((TENSOR - X_LO,)),
        ],
        compiler_params=pltpu.CompilerParams(vmem_limit_bytes=PROJECT_VMEM),
        cost_estimate=pl.CostEstimate(flops=2 * HALF * WIDTH * 256, bytes_accessed=4 << 20, transcendentals=0),
        name="project",
    )(x, wk, wv, gain, table)


def owners(slot_prompt_ref, owner_ref):
    core = lax.axis_index("core")
    prompts = slot_prompt_ref[...]
    row = jnp.zeros_like(prompts)
    for p in range(PROMPTS):
        row = jnp.where(prompts == p, owner_ref[:, p:p + 1], row)
    found = []
    for chip in range(CHIPS):
        first = chip * CORES * R_CAP
        found.append(
            [
                jnp.where(core == 0, row[0, first + r], row[0, first + R_CAP + r])
                for r in range(R_CAP)
            ]
        )
    return found


def select_kernel(slot_prompt_ref, owner_ref, mine_ref, other_ref, out_ref):
    found = owners(slot_prompt_ref, owner_ref)
    for chip in range(CHIPS):
        for r in range(R_CAP):
            q = found[chip][r]
            out_ref[chip, r, 0] = mine_ref[q, :UNIT]
            out_ref[chip, r, 1] = other_ref[q, :UNIT]


def select(slot_prompt, owner, mine, other):
    vmem = pl.BlockSpec(memory_space=pltpu.VMEM)
    return pl.pallas_call(
        select_kernel,
        in_specs=[vmem] * 4,
        out_specs=vmem,
        out_shape=jax.ShapeDtypeStruct((CHIPS, R_CAP, 2, UNIT, HEAD), bf16),
        compiler_params=pltpu.CompilerParams(vmem_limit_bytes=8 << 20),
        name="select",
    )(slot_prompt.reshape(1, -1), owner.reshape(1, -1), mine, other)


def attend_slot(core, length, live, kv_ref, q_ref, g_ref, rk_ref, rv_ref, dq_ref, drk_ref, drv_ref, grads_ref, ds_s, pb_s):
    ka, va = from_units(kv_ref[:, 0])
    kb, vb = from_units(kv_ref[:, 1])
    keys = jnp.concatenate([ka.astype(bf16), kb.astype(bf16), rk_ref[...]], axis=0)
    values = jnp.concatenate([va.astype(bf16), vb.astype(bf16), rv_ref[...]], axis=0)
    row = lax.broadcasted_iota(jnp.int32, (HALF, HEAD), 0)
    column = lax.broadcasted_iota(jnp.int32, (HALF, HEAD), 1)
    hidden = lambda first: jnp.where((column == 0) & (row + first >= length), FAR, 0.0)
    far = jnp.concatenate(
        [
            hidden(core * HALF),
            hidden((1 - core) * HALF),
            jnp.where((column == row) & (row > 0), FAR, 0.0),
        ],
        axis=0,
    ).astype(bf16)
    early = jnp.where((column == 0) | (column > row), 1.0, 0.0).astype(bf16)
    keys_far = jnp.concatenate([keys, far], axis=1)
    for h in range(0, GROUPS, PAIRS):
        cols = slice(h * HEAD, (h + PAIRS) * HEAD)
        stack = lambda ref: jnp.concatenate([ref[:, (h + i) * HEAD:(h + i + 1) * HEAD] for i in range(PAIRS)], axis=0)
        qh = jnp.concatenate([stack(q_ref), jnp.concatenate([early] * PAIRS, axis=0)], axis=1)
        st = dot_nt(keys_far, qh)
        dpt = dot_nt(values, stack(g_ref))
        top = jnp.max(st, axis=0, keepdims=True)
        e = jnp.exp2((st - top) * EXP2_SCALE)
        inv = 1.0 / jnp.sum(e, axis=0, keepdims=True)
        delta = jnp.sum(e * dpt, axis=0, keepdims=True) * inv
        p = e * inv
        pb_s[:, cols] = p.astype(bf16)
        ds_s[:, cols] = (p * (dpt - delta)).astype(bf16)
    rows_of = lambda ref: jnp.concatenate([ref[:, h * HEAD:(h + 1) * HEAD] for h in range(GROUPS)], axis=0)
    keep = jnp.where(live, 1.0, 0.0)
    kept = lambda x: x * keep
    dk = kept(dot_nn(ds_s[...], rows_of(q_ref)) * SCALE)
    dv = kept(dot_nn(pb_s[...], rows_of(g_ref)))
    grads_ref[:, 0] = to_units(dk[:HALF], dv[:HALF]).astype(bf16)
    grads_ref[:, 1] = to_units(dk[HALF:PLEN], dv[HALF:PLEN]).astype(bf16)
    drk_ref[...] = dk[PLEN:].astype(bf16)
    drv_ref[...] = dv[PLEN:].astype(bf16)
    keys_t = keys.T
    for h in range(GROUPS):
        cols = slice(h * HEAD, (h + 1) * HEAD)
        dq_ref[:, cols] = kept((dot_nn(keys_t, ds_s[:, cols]) * SCALE).T).astype(bf16)


def entry(ref, index):
    row = ref[...]
    here = lax.broadcasted_iota(jnp.int32, row.shape, 1) == index
    return jnp.sum(jnp.where(here, row, 0).astype(f32), axis=1, keepdims=True).astype(jnp.int32)


def attend_kernel(
    counts_ref, slot_prompt_ref, lengths_ref,
    kv_ref, q_ref, g_ref, rk_ref, rv_ref,
    dq_ref, drk_ref, drv_ref, grads_ref,
    ds_s, pb_s,
):
    core, dp = lax.axis_index("core"), lax.axis_index(DP)
    for slot in range(R_CAP):
        rows = pl.ds(slot * RLEN, RLEN)
        kv = kv_ref.at[:, slot]
        ins = [r.at[rows] for r in (q_ref, g_ref, rk_ref, rv_ref)]
        outs = [r.at[rows] for r in (dq_ref, drk_ref, drv_ref)] + [grads_ref.at[:, slot]]

        prompt = entry(slot_prompt_ref, dp * R_CAP + slot)
        length = entry(lengths_ref, prompt)
        live = entry(counts_ref, dp) > slot
        attend_slot(core, length, live, kv, *ins, *outs, ds_s.at[slot], pb_s.at[slot])


def attend(counts, slot_prompt, lengths, kv, q, g, rk, rv):
    width = GROUPS * HEAD
    vmem = pl.BlockSpec(memory_space=pltpu.VMEM)
    return pl.pallas_call(
        attend_kernel,
        in_specs=[vmem] * 8,
        out_specs=[vmem] * 4,
        out_shape=[
            jax.ShapeDtypeStruct((R_CAP * RLEN, width), bf16),
            jax.ShapeDtypeStruct((R_CAP * RLEN, HEAD), bf16),
            jax.ShapeDtypeStruct((R_CAP * RLEN, HEAD), bf16),
            jax.ShapeDtypeStruct((CHIPS, R_CAP, 2, UNIT, HEAD), bf16),
        ],
        scratch_shapes=[
            pltpu.VMEM((R_CAP, PLEN + RLEN, width), bf16),
            pltpu.VMEM((R_CAP, PLEN + RLEN, width), bf16),
        ],
        compiler_params=pltpu.CompilerParams(vmem_limit_bytes=16 << 20),
        cost_estimate=pl.CostEstimate(flops=10 * 2 * 384 * 1024 * 128, bytes_accessed=3 << 20, transcendentals=2 * 384 * 1024),
        name="attend",
    )(counts.reshape(1, -1), slot_prompt.reshape(1, -1), lengths.reshape(1, -1), kv, q, g, rk, rv)


def collect_kernel(slot_prompt_ref, owner_ref, got_ref, mine_ref, other_ref, acc):
    found = owners(slot_prompt_ref, owner_ref)
    acc[...] = jnp.zeros_like(acc)
    for chip in range(CHIPS):
        for r in range(R_CAP):
            q = found[chip][r]
            acc[q] += got_ref[chip, r].astype(f32)
    mine_ref[...] = acc[:, 0]
    other_ref[...] = acc[:, 1].astype(bf16)


def collect(slot_prompt, owner, got):
    vmem = pl.BlockSpec(memory_space=pltpu.VMEM)
    return pl.pallas_call(
        collect_kernel,
        in_specs=[vmem] * 3,
        out_specs=[vmem, vmem],
        out_shape=[
            jax.ShapeDtypeStruct((CHIPS, UNIT, HEAD), f32),
            jax.ShapeDtypeStruct((CHIPS, UNIT, HEAD), bf16),
        ],
        scratch_shapes=[pltpu.VMEM((CHIPS, 2, UNIT, HEAD), f32)],
        compiler_params=pltpu.CompilerParams(vmem_limit_bytes=8 << 20),
        name="collect",
    )(slot_prompt.reshape(1, -1), owner.reshape(1, -1), got)


def unkey_kernel(sum_ref, other_ref, units_ref, gain_ref, table_ref, out_ref):
    core, chip = lax.axis_index("core"), lax.axis_index(SPREAD)
    rows = pl.ds(pl.multiple_of(chip * PIECE, PIECE), PIECE)
    cos, sin = cos_sin(table_ref[core, rows])
    total = sum_ref[...] + other_ref[...].astype(f32)
    units = units_ref[...].astype(f32)
    dk, dv = total[:, :PIECE], total[:, PIECE:]
    raw = units[:, UNIT:UNIT + PIECE] + units[:, UNIT + PIECE:]
    inv = lax.rsqrt(jnp.mean(raw * raw, axis=-1, keepdims=True) + EPS)
    turned = swap_halves((dk * sin).reshape(HALF, HEAD)).reshape(CHIPS, PIECE, HEAD)
    dn = (dk * cos + turned) * gain_ref[...]
    dot = jnp.mean(raw * dn, axis=-1, keepdims=True)
    d_raw = inv * (dn - raw * (inv * inv * dot))
    out_ref[...] = jnp.concatenate(
        [d_raw.reshape(HALF, HEAD), dv.reshape(HALF, HEAD)], axis=1
    ).astype(bf16)


def unkey(sums, other, units, gain, table):
    vmem = pl.BlockSpec(memory_space=pltpu.VMEM)
    return pl.pallas_call(
        unkey_kernel,
        in_specs=[vmem] * 5,
        out_specs=vmem,
        out_shape=jax.ShapeDtypeStruct((HALF, 2 * HEAD), bf16),
        compiler_params=pltpu.CompilerParams(vmem_limit_bytes=8 << 20),
        name="unkey",
    )(sums, other, units, gain, table)


def input_grad_kernel(wk_ref, wv_ref, *refs):
    grads, got, out_ref = refs[:Y], refs[Y:2 * Y - 1], refs[-1]
    y = lax.axis_index("y")
    for half in range(X_LO):
        rows = pl.ds(pl.multiple_of((half * Y + y) * COLS, COLS), COLS)
        total = dot_nt(grads[0][...], jnp.concatenate([wk_ref[rows], wv_ref[rows]], axis=1))
        for k in range(1, Y):
            w = jnp.concatenate([got[k - 1][half, 0], got[k - 1][half, 1]], axis=1)
            total += dot_nt(grads[1 + LAST_FAR.index(k)][...], w)
        out_ref[:, half] = total.reshape(CHIPS, PIECE, COLS).astype(bf16)


def input_grad(wk, wv, grads, got):
    vmem = pl.BlockSpec(memory_space=pltpu.VMEM)
    return pl.pallas_call(
        input_grad_kernel,
        in_specs=[vmem] * (2 * Y + 1),
        out_specs=vmem,
        out_shape=jax.ShapeDtypeStruct((CHIPS, X_LO, PIECE, COLS), bf16),
        compiler_params=pltpu.CompilerParams(vmem_limit_bytes=16 << 20),
        cost_estimate=pl.CostEstimate(flops=2 * HALF * WIDTH * 256, bytes_accessed=4 << 20, transcendentals=0),
        name="input_grad",
    )(wk, wv, *grads, *got)


def together(first, second):
    flat, tree = jax.tree.flatten((first, second))
    return jax.tree.unflatten(tree, lax.optimization_barrier(flat))


def swap_y(x, k):
    return lax.ppermute(x, "y", [(i, i ^ k) for i in range(Y)])


def spread(x):
    return lax.all_to_all(x, SPREAD, 0, 0, tiled=True)


def swap_cores(x):
    return lax.ppermute(x, "core", [(0, 1), (1, 0)])


def on_device(
    prompt_x, key_matrix, value_matrix, k_gain, queries, response_keys, response_values,
    output_gradient, response_counts, slot_prompt, prompt_owner, prompt_lengths,
):
    table = rope_table()
    gain = k_gain.reshape(1, HEAD)
    with jax.named_scope("keys_out"):
        units, *send = project(prompt_x, key_matrix, value_matrix, gain, table)
        got = [swap_y(send[k - 1], k) for k in range(1, Y)]
        mine = spread(units)
        needed = select(slot_prompt, prompt_owner, mine, swap_cores(mine))
        needed, (got[0], got[2]) = together(spread(needed), (got[0], got[2]))
    with jax.named_scope("attention"):
        dq, drk, drv, grads = attend(
            response_counts, slot_prompt, prompt_lengths,
            needed, queries, output_gradient, response_keys, response_values,
        )
    with jax.named_scope("grads_back"):
        sums, other = collect(slot_prompt, prompt_owner, spread(grads))
        other, got[1] = together(other, got[1])
        both = unkey(sums, swap_cores(other), mine, gain, table)
        both = [both] + [swap_y(both, k) for k in LAST_FAR]
    with jax.named_scope("input_grad"):
        shares = input_grad(key_matrix, value_matrix, both, got)
        shares = shares.reshape(CHIPS * X_LO, PIECE, COLS)
        shares = lax.all_to_all(shares, SPREAD + ("x_lo",), 0, 0, tiled=True)
        shares = shares.reshape(CHIPS, X_LO, PIECE, COLS).astype(f32)
        d_prompt = jnp.sum(shares, axis=1).reshape(HALF, COLS).astype(bf16)
    return dq, drk, drv, d_prompt


def solution(mesh):
    fine = Mesh(mesh.devices.reshape(2, 8, 2, 2, 4), ("x_hi", "z", "core", "x_lo", "y"))
    dp, tensor = ("x_hi", "z", "core"), ("x_lo", "y")
    both = P(dp, tensor)
    return jax.shard_map(
        on_device,
        mesh=fine,
        in_specs=(P(dp, None), P(None, tensor), P(None, tensor), P(), both, both, both, both, P(), P(), P(), P()),
        out_specs=(both,) * 4,
        check_vma=False,
    )
```

```python
import functools

import jax
import jax.numpy as jnp
import numpy as np
from jax import lax
from jax.experimental import pallas as pl
from jax.experimental.pallas import tpu as pltpu
from jax.sharding import Mesh
from jax.sharding import PartitionSpec as P

HEAD = 128
R_CAP = 2
RLEN = 128
PLEN = 256
HALF = 128
CHIPS = 16
CORES = 2
PROMPTS = 16
PIECE = HALF // CHIPS
UNIT = 2 * PIECE
WIDTH = 5120
TENSOR = 8
COLS = WIDTH // TENSOR
GROUPS = 8
SCALE = HEAD ** (-0.5)
EXP2_SCALE = SCALE * float(np.log2(np.e))
EPS = 1e-06
FAR = -1e30
PAIRS = 2
f32 = jnp.float32
bf16 = jnp.bfloat16
DP = ("x_hi", "z", "core")
SPREAD = ("x_hi", "z")
X_LO = 2
Y = 4
PROJECT_VMEM = 60 << 20
LAST_FAR = (1, 3, 2)


def rope_table():
    freqs = 1000000.0 ** (-np.arange(HEAD // 2, dtype=np.float64) * 2.0 / HEAD)
    angles = np.arange(PLEN, dtype=np.float64)[:, None] * freqs[None, :]
    both = np.concatenate([np.cos(angles), np.sin(angles)], axis=1)
    return both.astype(np.float32).reshape(CORES, HALF, HEAD)


def cos_sin(table):
    first = lax.broadcasted_iota(jnp.int32, table.shape, 1) < HEAD // 2
    turned = swap_halves(table)
    return jnp.where(first, table, turned), jnp.where(first, -turned, table)


def swap_halves(u):
    return pltpu.roll(u, HEAD // 2, 1)


def to_units(keys, values):
    n = keys.shape[0] // PIECE
    return jnp.concatenate(
        [keys.reshape(n, PIECE, HEAD), values.reshape(n, PIECE, HEAD)], axis=1
    )


def from_units(units):
    u = units.astype(f32)
    n = u.shape[0]
    return u[:, :PIECE].reshape(n * PIECE, HEAD), u[:, PIECE:].reshape(n * PIECE, HEAD)


def dot_nn(a, b):
    return lax.dot_general(a, b, (((1,), (0,)), ((), ())), preferred_element_type=f32)


def dot_nt(a, b):
    return lax.dot_general(a, b, (((1,), (1,)), ((), ())), preferred_element_type=f32)


def project_kernel(
    x_ref, wk_ref, wv_ref, gain_ref, table_ref, units_ref, *refs
):
    send_refs, (x_s, w_s, table_s, gain_s, sems, small_sems, send_sems) = refs[:Y - 1], refs[Y - 1:]
    core, y = lax.axis_index("core"), lax.axis_index("y")
    order = [(k, half) for k in range(1, Y) for half in range(X_LO)] + [(0, 0), (0, 1)]
    copies = []
    for n, (k, half) in enumerate(order):
        rows = pl.ds(pl.multiple_of((half * Y + (y ^ k)) * COLS, COLS), COLS)
        copies.append(
            [
                pltpu.make_async_copy(wk_ref.at[rows], w_s.at[n, 0], sems.at[n, 1]),
                pltpu.make_async_copy(wv_ref.at[rows], w_s.at[n, 1], sems.at[n, 2]),
                pltpu.make_async_copy(x_ref.at[:, rows], x_s.at[n], sems.at[n, 0]),
            ]
        )
        for copy in copies[-1]:
            copy.start()
    small = [
        pltpu.make_async_copy(table_ref.at[core], table_s, small_sems.at[0]),
        pltpu.make_async_copy(gain_ref, gain_s, small_sems.at[1]),
    ]
    for copy in small:
        copy.start()
    sends = [
        pltpu.make_async_copy(w_s.at[n], send_refs[k - 1].at[half], send_sems.at[n])
        for n, (k, half) in enumerate(order)
        if k
    ]
    acc = jnp.zeros((HALF, 2 * HEAD), f32)
    for n in range(TENSOR):
        for copy in copies[n]:
            copy.wait()
        if n < len(sends):
            sends[n].start()
        acc += dot_nn(x_s[n], jnp.concatenate([w_s[n, 0], w_s[n, 1]], axis=1))
    for copy in small:
        copy.wait()
    cos, sin = cos_sin(table_s[...])
    raw = acc[:, :HEAD]
    inv = lax.rsqrt(jnp.mean(raw * raw, axis=-1, keepdims=True) + EPS)
    u = raw * inv * gain_s[...]
    keys = u * cos + swap_halves(u) * sin
    high = raw.astype(bf16).astype(f32)
    parts = [keys, acc[:, HEAD:], high, raw - high]
    units_ref[...] = jnp.concatenate(
        [part.reshape(CHIPS, PIECE, HEAD) for part in parts], axis=1
    ).astype(bf16)
    for copy in sends:
        copy.wait()


def project(x, wk, wv, gain, table):
    vmem = pl.BlockSpec(memory_space=pltpu.VMEM)
    hbm = pl.BlockSpec(memory_space=pltpu.HBM)
    anywhere = pl.BlockSpec(memory_space=pl.ANY)
    return pl.pallas_call(
        project_kernel,
        in_specs=[hbm] * 5,
        out_specs=[vmem] + [anywhere] * (Y - 1),
        out_shape=[jax.ShapeDtypeStruct((CHIPS, 2 * UNIT, HEAD), bf16)]
        + [jax.ShapeDtypeStruct((X_LO, 2, COLS, HEAD), bf16)] * (Y - 1),
        scratch_shapes=[
            pltpu.VMEM((TENSOR, HALF, COLS), bf16),
            pltpu.VMEM((TENSOR, 2, COLS, HEAD), bf16),
            pltpu.VMEM((HALF, HEAD), f32),
            pltpu.VMEM((1, HEAD), f32),
            pltpu.SemaphoreType.DMA((TENSOR, 3)),
            pltpu.SemaphoreType.DMA((2,)),
            pltpu.SemaphoreType.DMA((TENSOR - X_LO,)),
        ],
        compiler_params=pltpu.CompilerParams(vmem_limit_bytes=PROJECT_VMEM),
        cost_estimate=pl.CostEstimate(flops=2 * HALF * WIDTH * 256, bytes_accessed=4 << 20, transcendentals=0),
        name="project",
    )(x, wk, wv, gain, table)


def owners(slot_prompt_ref, owner_ref):
    core = lax.axis_index("core")
    prompts = slot_prompt_ref[...]
    row = jnp.zeros_like(prompts)
    for p in range(PROMPTS):
        row = jnp.where(prompts == p, owner_ref[:, p:p + 1], row)
    found = []
    for chip in range(CHIPS):
        first = chip * CORES * R_CAP
        found.append(
            [
                jnp.where(core == 0, row[0, first + r], row[0, first + R_CAP + r])
                for r in range(R_CAP)
            ]
        )
    return found


def select_kernel(slot_prompt_ref, owner_ref, mine_ref, other_ref, out_ref):
    found = owners(slot_prompt_ref, owner_ref)
    for chip in range(CHIPS):
        for r in range(R_CAP):
            q = found[chip][r]
            out_ref[chip, r, 0] = mine_ref[q, :UNIT]
            out_ref[chip, r, 1] = other_ref[q, :UNIT]


def select(slot_prompt, owner, mine, other):
    vmem = pl.BlockSpec(memory_space=pltpu.VMEM)
    return pl.pallas_call(
        select_kernel,
        in_specs=[vmem] * 4,
        out_specs=vmem,
        out_shape=jax.ShapeDtypeStruct((CHIPS, R_CAP, 2, UNIT, HEAD), bf16),
        compiler_params=pltpu.CompilerParams(vmem_limit_bytes=8 << 20),
        name="select",
    )(slot_prompt.reshape(1, -1), owner.reshape(1, -1), mine, other)


def attend_slot(core, length, live, kv_ref, q_ref, g_ref, rk_ref, rv_ref, dq_ref, drk_ref, drv_ref, grads_ref, ds_s, pb_s):
    ka, va = from_units(kv_ref[:, 0])
    kb, vb = from_units(kv_ref[:, 1])
    keys = jnp.concatenate([ka.astype(bf16), kb.astype(bf16), rk_ref[...]], axis=0)
    values = jnp.concatenate([va.astype(bf16), vb.astype(bf16), rv_ref[...]], axis=0)
    row = lax.broadcasted_iota(jnp.int32, (HALF, HEAD), 0)
    column = lax.broadcasted_iota(jnp.int32, (HALF, HEAD), 1)
    hidden = lambda first: jnp.where((column == 0) & (row + first >= length), FAR, 0.0)
    far = jnp.concatenate(
        [
            hidden(core * HALF),
            hidden((1 - core) * HALF),
            jnp.where((column == row) & (row > 0), FAR, 0.0),
        ],
        axis=0,
    ).astype(bf16)
    early = jnp.where((column == 0) | (column > row), 1.0, 0.0).astype(bf16)
    keys_far = jnp.concatenate([keys, far], axis=1)
    for h in range(0, GROUPS, PAIRS):
        cols = slice(h * HEAD, (h + PAIRS) * HEAD)
        stack = lambda ref: jnp.concatenate([ref[:, (h + i) * HEAD:(h + i + 1) * HEAD] for i in range(PAIRS)], axis=0)
        qh = jnp.concatenate([stack(q_ref), jnp.concatenate([early] * PAIRS, axis=0)], axis=1)
        st = dot_nt(keys_far, qh)
        dpt = dot_nt(values, stack(g_ref))
        top = jnp.max(st, axis=0, keepdims=True)
        e = jnp.exp2((st - top) * EXP2_SCALE)
        inv = 1.0 / jnp.sum(e, axis=0, keepdims=True)
        delta = jnp.sum(e * dpt, axis=0, keepdims=True) * inv
        p = e * inv
        pb_s[:, cols] = p.astype(bf16)
        ds_s[:, cols] = (p * (dpt - delta)).astype(bf16)
    rows_of = lambda ref: jnp.concatenate([ref[:, h * HEAD:(h + 1) * HEAD] for h in range(GROUPS)], axis=0)
    keep = jnp.where(live, 1.0, 0.0)
    kept = lambda x: x * keep
    dk = kept(dot_nn(ds_s[...], rows_of(q_ref)) * SCALE)
    dv = kept(dot_nn(pb_s[...], rows_of(g_ref)))
    grads_ref[:, 0] = to_units(dk[:HALF], dv[:HALF]).astype(bf16)
    grads_ref[:, 1] = to_units(dk[HALF:PLEN], dv[HALF:PLEN]).astype(bf16)
    drk_ref[...] = dk[PLEN:].astype(bf16)
    drv_ref[...] = dv[PLEN:].astype(bf16)
    keys_t = keys.T
    for h in range(GROUPS):
        cols = slice(h * HEAD, (h + 1) * HEAD)
        dq_ref[:, cols] = kept((dot_nn(keys_t, ds_s[:, cols]) * SCALE).T).astype(bf16)


def entry(ref, index):
    row = ref[...]
    here = lax.broadcasted_iota(jnp.int32, row.shape, 1) == index
    return jnp.sum(jnp.where(here, row, 0).astype(f32), axis=1, keepdims=True).astype(jnp.int32)


def attend_kernel(
    counts_ref, slot_prompt_ref, lengths_ref,
    kv_ref, q_ref, g_ref, rk_ref, rv_ref,
    dq_ref, drk_ref, drv_ref, grads_ref,
    ds_s, pb_s,
):
    core, dp = lax.axis_index("core"), lax.axis_index(DP)
    for slot in range(R_CAP):
        rows = pl.ds(slot * RLEN, RLEN)
        kv = kv_ref.at[:, slot]
        ins = [r.at[rows] for r in (q_ref, g_ref, rk_ref, rv_ref)]
        outs = [r.at[rows] for r in (dq_ref, drk_ref, drv_ref)] + [grads_ref.at[:, slot]]

        prompt = entry(slot_prompt_ref, dp * R_CAP + slot)
        length = entry(lengths_ref, prompt)
        live = entry(counts_ref, dp) > slot
        attend_slot(core, length, live, kv, *ins, *outs, ds_s.at[slot], pb_s.at[slot])


def attend(counts, slot_prompt, lengths, kv, q, g, rk, rv):
    width = GROUPS * HEAD
    vmem = pl.BlockSpec(memory_space=pltpu.VMEM)
    return pl.pallas_call(
        attend_kernel,
        in_specs=[vmem] * 8,
        out_specs=[vmem] * 4,
        out_shape=[
            jax.ShapeDtypeStruct((R_CAP * RLEN, width), bf16),
            jax.ShapeDtypeStruct((R_CAP * RLEN, HEAD), bf16),
            jax.ShapeDtypeStruct((R_CAP * RLEN, HEAD), bf16),
            jax.ShapeDtypeStruct((CHIPS, R_CAP, 2, UNIT, HEAD), bf16),
        ],
        scratch_shapes=[
            pltpu.VMEM((R_CAP, PLEN + RLEN, width), bf16),
            pltpu.VMEM((R_CAP, PLEN + RLEN, width), bf16),
        ],
        compiler_params=pltpu.CompilerParams(vmem_limit_bytes=16 << 20),
        cost_estimate=pl.CostEstimate(flops=10 * 2 * 384 * 1024 * 128, bytes_accessed=3 << 20, transcendentals=2 * 384 * 1024),
        name="attend",
    )(counts.reshape(1, -1), slot_prompt.reshape(1, -1), lengths.reshape(1, -1), kv, q, g, rk, rv)


def collect_kernel(slot_prompt_ref, owner_ref, got_ref, mine_ref, other_ref, acc):
    found = owners(slot_prompt_ref, owner_ref)
    acc[...] = jnp.zeros_like(acc)
    for chip in range(CHIPS):
        for r in range(R_CAP):
            q = found[chip][r]
            acc[q] += got_ref[chip, r].astype(f32)
    mine_ref[...] = acc[:, 0]
    other_ref[...] = acc[:, 1].astype(bf16)


def collect(slot_prompt, owner, got):
    vmem = pl.BlockSpec(memory_space=pltpu.VMEM)
    return pl.pallas_call(
        collect_kernel,
        in_specs=[vmem] * 3,
        out_specs=[vmem, vmem],
        out_shape=[
            jax.ShapeDtypeStruct((CHIPS, UNIT, HEAD), f32),
            jax.ShapeDtypeStruct((CHIPS, UNIT, HEAD), bf16),
        ],
        scratch_shapes=[pltpu.VMEM((CHIPS, 2, UNIT, HEAD), f32)],
        compiler_params=pltpu.CompilerParams(vmem_limit_bytes=8 << 20),
        name="collect",
    )(slot_prompt.reshape(1, -1), owner.reshape(1, -1), got)


def unkey_kernel(sum_ref, other_ref, units_ref, gain_ref, table_ref, out_ref):
    core, chip = lax.axis_index("core"), lax.axis_index(SPREAD)
    rows = pl.ds(pl.multiple_of(chip * PIECE, PIECE), PIECE)
    cos, sin = cos_sin(table_ref[core, rows])
    total = sum_ref[...] + other_ref[...].astype(f32)
    units = units_ref[...].astype(f32)
    dk, dv = total[:, :PIECE], total[:, PIECE:]
    raw = units[:, UNIT:UNIT + PIECE] + units[:, UNIT + PIECE:]
    inv = lax.rsqrt(jnp.mean(raw * raw, axis=-1, keepdims=True) + EPS)
    turned = swap_halves((dk * sin).reshape(HALF, HEAD)).reshape(CHIPS, PIECE, HEAD)
    dn = (dk * cos + turned) * gain_ref[...]
    dot = jnp.mean(raw * dn, axis=-1, keepdims=True)
    d_raw = inv * (dn - raw * (inv * inv * dot))
    out_ref[...] = jnp.concatenate(
        [d_raw.reshape(HALF, HEAD), dv.reshape(HALF, HEAD)], axis=1
    ).astype(bf16)


def unkey(sums, other, units, gain, table):
    vmem = pl.BlockSpec(memory_space=pltpu.VMEM)
    return pl.pallas_call(
        unkey_kernel,
        in_specs=[vmem] * 5,
        out_specs=vmem,
        out_shape=jax.ShapeDtypeStruct((HALF, 2 * HEAD), bf16),
        compiler_params=pltpu.CompilerParams(vmem_limit_bytes=8 << 20),
        name="unkey",
    )(sums, other, units, gain, table)


def input_grad_kernel(wk_ref, wv_ref, *refs):
    grads, got, out_ref = refs[:Y], refs[Y:2 * Y - 1], refs[-1]
    y = lax.axis_index("y")
    for half in range(X_LO):
        rows = pl.ds(pl.multiple_of((half * Y + y) * COLS, COLS), COLS)
        total = dot_nt(grads[0][...], jnp.concatenate([wk_ref[rows], wv_ref[rows]], axis=1))
        for k in range(1, Y):
            w = jnp.concatenate([got[k - 1][half, 0], got[k - 1][half, 1]], axis=1)
            total += dot_nt(grads[1 + LAST_FAR.index(k)][...], w)
        out_ref[half] = total.reshape(CHIPS, PIECE, COLS).astype(bf16)


def input_grad(wk, wv, grads, got):
    vmem = pl.BlockSpec(memory_space=pltpu.VMEM)
    return pl.pallas_call(
        input_grad_kernel,
        in_specs=[vmem] * (2 * Y + 1),
        out_specs=vmem,
        out_shape=jax.ShapeDtypeStruct((X_LO, CHIPS, PIECE, COLS), bf16),
        compiler_params=pltpu.CompilerParams(vmem_limit_bytes=16 << 20),
        cost_estimate=pl.CostEstimate(flops=2 * HALF * WIDTH * 256, bytes_accessed=4 << 20, transcendentals=0),
        name="input_grad",
    )(wk, wv, *grads, *got)


def together(first, second):
    flat, tree = jax.tree.flatten((first, second))
    return jax.tree.unflatten(tree, lax.optimization_barrier(flat))


def swap_y(x, k):
    return lax.ppermute(x, "y", [(i, i ^ k) for i in range(Y)])


def spread(x):
    return lax.all_to_all(x, SPREAD, 0, 0, tiled=True)


def swap_cores(x):
    return lax.ppermute(x, "core", [(0, 1), (1, 0)])


def on_device(
    prompt_x, key_matrix, value_matrix, k_gain, queries, response_keys, response_values,
    output_gradient, response_counts, slot_prompt, prompt_owner, prompt_lengths,
):
    table = rope_table()
    gain = k_gain.reshape(1, HEAD)
    with jax.named_scope("keys_out"):
        units, *send = project(prompt_x, key_matrix, value_matrix, gain, table)
        got = [swap_y(send[k - 1], k) for k in range(1, Y)]
        mine = spread(units)
        needed = select(slot_prompt, prompt_owner, mine, swap_cores(mine))
        needed, (got[0], got[2]) = together(spread(needed), (got[0], got[2]))
    with jax.named_scope("attention"):
        dq, drk, drv, grads = attend(
            response_counts, slot_prompt, prompt_lengths,
            needed, queries, output_gradient, response_keys, response_values,
        )
    with jax.named_scope("grads_back"):
        sums, other = collect(slot_prompt, prompt_owner, spread(grads))
        other, got[1] = together(other, got[1])
        both = unkey(sums, swap_cores(other), mine, gain, table)
        both = [both] + [swap_y(both, k) for k in LAST_FAR]
    with jax.named_scope("input_grad"):
        shares = input_grad(key_matrix, value_matrix, both, got)
        shares = shares.reshape(X_LO * CHIPS, PIECE, COLS)
        shares = lax.all_to_all(shares, ("x_lo",) + SPREAD, 0, 0, tiled=True)
        shares = shares.reshape(X_LO, CHIPS, PIECE, COLS).astype(f32)
        d_prompt = jnp.sum(shares, axis=0).reshape(HALF, COLS).astype(bf16)
    return dq, drk, drv, d_prompt


def solution(mesh):
    fine = Mesh(mesh.devices.reshape(2, 8, 2, 2, 4), ("x_hi", "z", "core", "x_lo", "y"))
    dp, tensor = ("x_hi", "z", "core"), ("x_lo", "y")
    both = P(dp, tensor)
    return jax.shard_map(
        on_device,
        mesh=fine,
        in_specs=(P(dp, None), P(None, tensor), P(None, tensor), P(), both, both, both, both, P(), P(), P(), P()),
        out_specs=(both,) * 4,
        check_vma=False,
    )
```

```python
import functools

import jax
import jax.numpy as jnp
import numpy as np
from jax import lax
from jax.experimental import pallas as pl
from jax.experimental.pallas import tpu as pltpu
from jax.sharding import Mesh
from jax.sharding import PartitionSpec as P

HEAD = 128
R_CAP = 2
RLEN = 128
PLEN = 256
HALF = 128
CHIPS = 16
CORES = 2
PROMPTS = 16
PIECE = HALF // CHIPS
UNIT = 2 * PIECE
WIDTH = 5120
TENSOR = 8
COLS = WIDTH // TENSOR
GROUPS = 8
SCALE = HEAD ** (-0.5)
EXP2_SCALE = SCALE * float(np.log2(np.e))
EPS = 1e-06
FAR = -1e30
PAIRS = 2
f32 = jnp.float32
bf16 = jnp.bfloat16
DP = ("x_hi", "z", "core")
SPREAD = ("x_hi", "z")
X_LO = 2
Y = 4
PROJECT_VMEM = 60 << 20
LAST_FAR = (1, 3, 2)


def rope_table():
    freqs = 1000000.0 ** (-np.arange(HEAD // 2, dtype=np.float64) * 2.0 / HEAD)
    angles = np.arange(PLEN, dtype=np.float64)[:, None] * freqs[None, :]
    both = np.concatenate([np.cos(angles), np.sin(angles)], axis=1)
    return both.astype(np.float32).reshape(CORES, HALF, HEAD)


def cos_sin(table):
    first = lax.broadcasted_iota(jnp.int32, table.shape, 1) < HEAD // 2
    turned = swap_halves(table)
    return jnp.where(first, table, turned), jnp.where(first, -turned, table)


def swap_halves(u):
    return pltpu.roll(u, HEAD // 2, 1)


def to_units(keys, values):
    n = keys.shape[0] // PIECE
    return jnp.concatenate(
        [keys.reshape(n, PIECE, HEAD), values.reshape(n, PIECE, HEAD)], axis=1
    )


def from_units(units):
    u = units.astype(f32)
    n = u.shape[0]
    return u[:, :PIECE].reshape(n * PIECE, HEAD), u[:, PIECE:].reshape(n * PIECE, HEAD)


def dot_nn(a, b):
    return lax.dot_general(a, b, (((1,), (0,)), ((), ())), preferred_element_type=f32)


def dot_nt(a, b):
    return lax.dot_general(a, b, (((1,), (1,)), ((), ())), preferred_element_type=f32)


def project_kernel(
    x_ref, wk_ref, wv_ref, gain_ref, table_ref, units_ref, *refs
):
    send_refs, (x_s, w_s, table_s, gain_s, sems, small_sems, send_sems) = refs[:Y - 1], refs[Y - 1:]
    core, y = lax.axis_index("core"), lax.axis_index("y")
    order = [(k, half) for k in range(1, Y) for half in range(X_LO)] + [(0, 0), (0, 1)]
    copies = []
    for n, (k, half) in enumerate(order):
        rows = pl.ds(pl.multiple_of((half * Y + (y ^ k)) * COLS, COLS), COLS)
        copies.append(
            [
                pltpu.make_async_copy(wk_ref.at[rows], w_s.at[n, 0], sems.at[n, 1]),
                pltpu.make_async_copy(wv_ref.at[rows], w_s.at[n, 1], sems.at[n, 2]),
                pltpu.make_async_copy(x_ref.at[:, rows], x_s.at[n], sems.at[n, 0]),
            ]
        )
        for copy in copies[-1]:
            copy.start()
    small = [
        pltpu.make_async_copy(table_ref.at[core], table_s, small_sems.at[0]),
        pltpu.make_async_copy(gain_ref, gain_s, small_sems.at[1]),
    ]
    for copy in small:
        copy.start()
    sends = [
        pltpu.make_async_copy(w_s.at[n], send_refs[k - 1].at[half], send_sems.at[n])
        for n, (k, half) in enumerate(order)
        if k
    ]
    acc = jnp.zeros((HALF, 2 * HEAD), f32)
    for n in range(TENSOR):
        for copy in copies[n]:
            copy.wait()
        if n < len(sends):
            sends[n].start()
        acc += dot_nn(x_s[n], jnp.concatenate([w_s[n, 0], w_s[n, 1]], axis=1))
    for copy in small:
        copy.wait()
    cos, sin = cos_sin(table_s[...])
    raw = acc[:, :HEAD]
    inv = lax.rsqrt(jnp.mean(raw * raw, axis=-1, keepdims=True) + EPS)
    u = raw * inv * gain_s[...]
    keys = u * cos + swap_halves(u) * sin
    high = raw.astype(bf16).astype(f32)
    parts = [keys, acc[:, HEAD:], high, raw - high]
    units_ref[...] = jnp.concatenate(
        [part.reshape(CHIPS, PIECE, HEAD) for part in parts], axis=1
    ).astype(bf16)
    for copy in sends:
        copy.wait()


def project(x, wk, wv, gain, table):
    vmem = pl.BlockSpec(memory_space=pltpu.VMEM)
    hbm = pl.BlockSpec(memory_space=pltpu.HBM)
    anywhere = pl.BlockSpec(memory_space=pl.ANY)
    return pl.pallas_call(
        project_kernel,
        in_specs=[hbm] * 5,
        out_specs=[vmem] + [anywhere] * (Y - 1),
        out_shape=[jax.ShapeDtypeStruct((CHIPS, 2 * UNIT, HEAD), bf16)]
        + [jax.ShapeDtypeStruct((X_LO, 2, COLS, HEAD), bf16)] * (Y - 1),
        scratch_shapes=[
            pltpu.VMEM((TENSOR, HALF, COLS), bf16),
            pltpu.VMEM((TENSOR, 2, COLS, HEAD), bf16),
            pltpu.VMEM((HALF, HEAD), f32),
            pltpu.VMEM((1, HEAD), f32),
            pltpu.SemaphoreType.DMA((TENSOR, 3)),
            pltpu.SemaphoreType.DMA((2,)),
            pltpu.SemaphoreType.DMA((TENSOR - X_LO,)),
        ],
        compiler_params=pltpu.CompilerParams(vmem_limit_bytes=PROJECT_VMEM),
        cost_estimate=pl.CostEstimate(flops=2 * HALF * WIDTH * 256, bytes_accessed=4 << 20, transcendentals=0),
        name="project",
    )(x, wk, wv, gain, table)


def owners(slot_prompt_ref, owner_ref):
    core = lax.axis_index("core")
    prompts = slot_prompt_ref[...]
    row = jnp.zeros_like(prompts)
    for p in range(PROMPTS):
        row = jnp.where(prompts == p, owner_ref[:, p:p + 1], row)
    found = []
    for chip in range(CHIPS):
        first = chip * CORES * R_CAP
        found.append(
            [
                jnp.where(core == 0, row[0, first + r], row[0, first + R_CAP + r])
                for r in range(R_CAP)
            ]
        )
    return found


def select_kernel(slot_prompt_ref, owner_ref, mine_ref, other_ref, out_ref):
    found = owners(slot_prompt_ref, owner_ref)
    for chip in range(CHIPS):
        for r in range(R_CAP):
            q = found[chip][r]
            out_ref[chip, r, 0] = mine_ref[q, :UNIT]
            out_ref[chip, r, 1] = other_ref[q, :UNIT]


def select(slot_prompt, owner, mine, other):
    vmem = pl.BlockSpec(memory_space=pltpu.VMEM)
    return pl.pallas_call(
        select_kernel,
        in_specs=[vmem] * 4,
        out_specs=vmem,
        out_shape=jax.ShapeDtypeStruct((CHIPS, R_CAP, 2, UNIT, HEAD), bf16),
        compiler_params=pltpu.CompilerParams(vmem_limit_bytes=8 << 20),
        name="select",
    )(slot_prompt.reshape(1, -1), owner.reshape(1, -1), mine, other)


def attend_slot(core, length, live, kv_ref, q_ref, g_ref, rk_ref, rv_ref, dq_ref, drk_ref, drv_ref, grads_ref, ds_s, pb_s):
    ka, va = from_units(kv_ref[:, 0])
    kb, vb = from_units(kv_ref[:, 1])
    keys = jnp.concatenate([ka.astype(bf16), kb.astype(bf16), rk_ref[...]], axis=0)
    values = jnp.concatenate([va.astype(bf16), vb.astype(bf16), rv_ref[...]], axis=0)
    row = lax.broadcasted_iota(jnp.int32, (HALF, HEAD), 0)
    column = lax.broadcasted_iota(jnp.int32, (HALF, HEAD), 1)
    hidden = lambda first: jnp.where((column == 0) & (row + first >= length), FAR, 0.0)
    far = jnp.concatenate(
        [
            hidden(core * HALF),
            hidden((1 - core) * HALF),
            jnp.where((column == row) & (row > 0), FAR, 0.0),
        ],
        axis=0,
    ).astype(bf16)
    early = jnp.where((column == 0) | (column > row), 1.0, 0.0).astype(bf16)
    keys_far = jnp.concatenate([keys, far], axis=1)
    for h in range(0, GROUPS, PAIRS):
        cols = slice(h * HEAD, (h + PAIRS) * HEAD)
        stack = lambda ref: jnp.concatenate([ref[:, (h + i) * HEAD:(h + i + 1) * HEAD] for i in range(PAIRS)], axis=0)
        qh = jnp.concatenate([stack(q_ref), jnp.concatenate([early] * PAIRS, axis=0)], axis=1)
        st = dot_nt(keys_far, qh)
        dpt = dot_nt(values, stack(g_ref))
        top = jnp.max(st, axis=0, keepdims=True)
        e = jnp.exp2((st - top) * EXP2_SCALE)
        inv = 1.0 / jnp.sum(e, axis=0, keepdims=True)
        delta = jnp.sum(e * dpt, axis=0, keepdims=True) * inv
        p = e * inv
        pb_s[:, cols] = p.astype(bf16)
        ds_s[:, cols] = (p * (dpt - delta)).astype(bf16)
    rows_of = lambda ref: jnp.concatenate([ref[:, h * HEAD:(h + 1) * HEAD] for h in range(GROUPS)], axis=0)
    keep = jnp.where(live, 1.0, 0.0)
    kept = lambda x: x * keep
    dk = kept(dot_nn(ds_s[...], rows_of(q_ref)) * SCALE)
    dv = kept(dot_nn(pb_s[...], rows_of(g_ref)))
    grads_ref[:, 0] = to_units(dk[:HALF], dv[:HALF]).astype(bf16)
    grads_ref[:, 1] = to_units(dk[HALF:PLEN], dv[HALF:PLEN]).astype(bf16)
    drk_ref[...] = dk[PLEN:].astype(bf16)
    drv_ref[...] = dv[PLEN:].astype(bf16)
    keys_t = keys.T
    for h in range(0, GROUPS, PAIRS):
        d_q = kept(dot_nn(keys_t, ds_s[:, h * HEAD:(h + PAIRS) * HEAD]) * SCALE)
        for i in range(PAIRS):
            dq_ref[:, (h + i) * HEAD:(h + i + 1) * HEAD] = d_q[:, i * HEAD:(i + 1) * HEAD].T.astype(bf16)


def entry(ref, index):
    row = ref[...]
    here = lax.broadcasted_iota(jnp.int32, row.shape, 1) == index
    return jnp.sum(jnp.where(here, row, 0).astype(f32), axis=1, keepdims=True).astype(jnp.int32)


def attend_kernel(
    counts_ref, slot_prompt_ref, lengths_ref,
    kv_ref, q_ref, g_ref, rk_ref, rv_ref,
    dq_ref, drk_ref, drv_ref, grads_ref,
    ds_s, pb_s,
):
    core, dp = lax.axis_index("core"), lax.axis_index(DP)
    for slot in range(R_CAP):
        rows = pl.ds(slot * RLEN, RLEN)
        kv = kv_ref.at[:, slot]
        ins = [r.at[rows] for r in (q_ref, g_ref, rk_ref, rv_ref)]
        outs = [r.at[rows] for r in (dq_ref, drk_ref, drv_ref)] + [grads_ref.at[:, slot]]

        prompt = entry(slot_prompt_ref, dp * R_CAP + slot)
        length = entry(lengths_ref, prompt)
        live = entry(counts_ref, dp) > slot
        attend_slot(core, length, live, kv, *ins, *outs, ds_s.at[slot], pb_s.at[slot])


def attend(counts, slot_prompt, lengths, kv, q, g, rk, rv):
    width = GROUPS * HEAD
    vmem = pl.BlockSpec(memory_space=pltpu.VMEM)
    return pl.pallas_call(
        attend_kernel,
        in_specs=[vmem] * 8,
        out_specs=[vmem] * 4,
        out_shape=[
            jax.ShapeDtypeStruct((R_CAP * RLEN, width), bf16),
            jax.ShapeDtypeStruct((R_CAP * RLEN, HEAD), bf16),
            jax.ShapeDtypeStruct((R_CAP * RLEN, HEAD), bf16),
            jax.ShapeDtypeStruct((CHIPS, R_CAP, 2, UNIT, HEAD), bf16),
        ],
        scratch_shapes=[
            pltpu.VMEM((R_CAP, PLEN + RLEN, width), bf16),
            pltpu.VMEM((R_CAP, PLEN + RLEN, width), bf16),
        ],
        compiler_params=pltpu.CompilerParams(vmem_limit_bytes=16 << 20),
        cost_estimate=pl.CostEstimate(flops=10 * 2 * 384 * 1024 * 128, bytes_accessed=3 << 20, transcendentals=2 * 384 * 1024),
        name="attend",
    )(counts.reshape(1, -1), slot_prompt.reshape(1, -1), lengths.reshape(1, -1), kv, q, g, rk, rv)


def collect_kernel(slot_prompt_ref, owner_ref, got_ref, mine_ref, other_ref, acc):
    found = owners(slot_prompt_ref, owner_ref)
    acc[...] = jnp.zeros_like(acc)
    for chip in range(CHIPS):
        for r in range(R_CAP):
            q = found[chip][r]
            acc[q] += got_ref[chip, r].astype(f32)
    mine_ref[...] = acc[:, 0]
    other_ref[...] = acc[:, 1].astype(bf16)


def collect(slot_prompt, owner, got):
    vmem = pl.BlockSpec(memory_space=pltpu.VMEM)
    return pl.pallas_call(
        collect_kernel,
        in_specs=[vmem] * 3,
        out_specs=[vmem, vmem],
        out_shape=[
            jax.ShapeDtypeStruct((CHIPS, UNIT, HEAD), f32),
            jax.ShapeDtypeStruct((CHIPS, UNIT, HEAD), bf16),
        ],
        scratch_shapes=[pltpu.VMEM((CHIPS, 2, UNIT, HEAD), f32)],
        compiler_params=pltpu.CompilerParams(vmem_limit_bytes=8 << 20),
        name="collect",
    )(slot_prompt.reshape(1, -1), owner.reshape(1, -1), got)


def unkey_kernel(sum_ref, other_ref, units_ref, gain_ref, table_ref, out_ref):
    core, chip = lax.axis_index("core"), lax.axis_index(SPREAD)
    rows = pl.ds(pl.multiple_of(chip * PIECE, PIECE), PIECE)
    cos, sin = cos_sin(table_ref[core, rows])
    total = sum_ref[...] + other_ref[...].astype(f32)
    units = units_ref[...].astype(f32)
    dk, dv = total[:, :PIECE], total[:, PIECE:]
    raw = units[:, UNIT:UNIT + PIECE] + units[:, UNIT + PIECE:]
    inv = lax.rsqrt(jnp.mean(raw * raw, axis=-1, keepdims=True) + EPS)
    turned = swap_halves((dk * sin).reshape(HALF, HEAD)).reshape(CHIPS, PIECE, HEAD)
    dn = (dk * cos + turned) * gain_ref[...]
    dot = jnp.mean(raw * dn, axis=-1, keepdims=True)
    d_raw = inv * (dn - raw * (inv * inv * dot))
    out_ref[...] = jnp.concatenate(
        [d_raw.reshape(HALF, HEAD), dv.reshape(HALF, HEAD)], axis=1
    ).astype(bf16)


def unkey(sums, other, units, gain, table):
    vmem = pl.BlockSpec(memory_space=pltpu.VMEM)
    return pl.pallas_call(
        unkey_kernel,
        in_specs=[vmem] * 5,
        out_specs=vmem,
        out_shape=jax.ShapeDtypeStruct((HALF, 2 * HEAD), bf16),
        compiler_params=pltpu.CompilerParams(vmem_limit_bytes=8 << 20),
        name="unkey",
    )(sums, other, units, gain, table)


def input_grad_kernel(wk_ref, wv_ref, *refs):
    grads, got, out_ref = refs[:Y], refs[Y:2 * Y - 1], refs[-1]
    y = lax.axis_index("y")
    for half in range(X_LO):
        rows = pl.ds(pl.multiple_of((half * Y + y) * COLS, COLS), COLS)
        total = dot_nt(grads[0][...], jnp.concatenate([wk_ref[rows], wv_ref[rows]], axis=1))
        for k in range(1, Y):
            w = jnp.concatenate([got[k - 1][half, 0], got[k - 1][half, 1]], axis=1)
            total += dot_nt(grads[1 + LAST_FAR.index(k)][...], w)
        out_ref[half] = total.reshape(CHIPS, PIECE, COLS).astype(bf16)


def input_grad(wk, wv, grads, got):
    vmem = pl.BlockSpec(memory_space=pltpu.VMEM)
    return pl.pallas_call(
        input_grad_kernel,
        in_specs=[vmem] * (2 * Y + 1),
        out_specs=vmem,
        out_shape=jax.ShapeDtypeStruct((X_LO, CHIPS, PIECE, COLS), bf16),
        compiler_params=pltpu.CompilerParams(vmem_limit_bytes=16 << 20),
        cost_estimate=pl.CostEstimate(flops=2 * HALF * WIDTH * 256, bytes_accessed=4 << 20, transcendentals=0),
        name="input_grad",
    )(wk, wv, *grads, *got)


def together(first, second):
    flat, tree = jax.tree.flatten((first, second))
    return jax.tree.unflatten(tree, lax.optimization_barrier(flat))


def swap_y(x, k):
    return lax.ppermute(x, "y", [(i, i ^ k) for i in range(Y)])


def spread(x):
    return lax.all_to_all(x, SPREAD, 0, 0, tiled=True)


def swap_cores(x):
    return lax.ppermute(x, "core", [(0, 1), (1, 0)])


def on_device(
    prompt_x, key_matrix, value_matrix, k_gain, queries, response_keys, response_values,
    output_gradient, response_counts, slot_prompt, prompt_owner, prompt_lengths,
):
    table = rope_table()
    gain = k_gain.reshape(1, HEAD)
    with jax.named_scope("keys_out"):
        units, *send = project(prompt_x, key_matrix, value_matrix, gain, table)
        got = [swap_y(send[k - 1], k) for k in range(1, Y)]
        mine = spread(units)
        needed = select(slot_prompt, prompt_owner, mine, swap_cores(mine))
        needed, (got[0], got[2]) = together(spread(needed), (got[0], got[2]))
    with jax.named_scope("attention"):
        dq, drk, drv, grads = attend(
            response_counts, slot_prompt, prompt_lengths,
            needed, queries, output_gradient, response_keys, response_values,
        )
    with jax.named_scope("grads_back"):
        sums, other = collect(slot_prompt, prompt_owner, spread(grads))
        other, got[1] = together(other, got[1])
        both = unkey(sums, swap_cores(other), mine, gain, table)
        both = [both] + [swap_y(both, k) for k in LAST_FAR]
    with jax.named_scope("input_grad"):
        shares = input_grad(key_matrix, value_matrix, both, got)
        shares = shares.reshape(X_LO * CHIPS, PIECE, COLS)
        shares = lax.all_to_all(shares, ("x_lo",) + SPREAD, 0, 0, tiled=True)
        shares = shares.reshape(X_LO, CHIPS, PIECE, COLS).astype(f32)
        d_prompt = jnp.sum(shares, axis=0).reshape(HALF, COLS).astype(bf16)
    return dq, drk, drv, d_prompt


def solution(mesh):
    fine = Mesh(mesh.devices.reshape(2, 8, 2, 2, 4), ("x_hi", "z", "core", "x_lo", "y"))
    dp, tensor = ("x_hi", "z", "core"), ("x_lo", "y")
    both = P(dp, tensor)
    return jax.shard_map(
        on_device,
        mesh=fine,
        in_specs=(P(dp, None), P(None, tensor), P(None, tensor), P(), both, both, both, both, P(), P(), P(), P()),
        out_specs=(both,) * 4,
        check_vma=False,
    )
```

```python
import functools

import jax
import jax.numpy as jnp
import numpy as np
from jax import lax
from jax.experimental import pallas as pl
from jax.experimental.pallas import tpu as pltpu
from jax.sharding import Mesh
from jax.sharding import PartitionSpec as P

HEAD = 128
R_CAP = 2
RLEN = 128
PLEN = 256
HALF = 128
CHIPS = 16
CORES = 2
PROMPTS = 16
PIECE = HALF // CHIPS
UNIT = 2 * PIECE
WIDTH = 5120
TENSOR = 8
COLS = WIDTH // TENSOR
GROUPS = 8
SCALE = HEAD ** (-0.5)
EXP2_SCALE = SCALE * float(np.log2(np.e))
EPS = 1e-06
FAR = -1e30
PAIRS = 2
f32 = jnp.float32
bf16 = jnp.bfloat16
DP = ("x_hi", "z", "core")
SPREAD = ("x_hi", "z")
X_LO = 2
Y = 4
PROJECT_VMEM = 60 << 20
LAST_FAR = (1, 3, 2)


def rope_table():
    freqs = 1000000.0 ** (-np.arange(HEAD // 2, dtype=np.float64) * 2.0 / HEAD)
    angles = np.arange(PLEN, dtype=np.float64)[:, None] * freqs[None, :]
    both = np.concatenate([np.cos(angles), np.sin(angles)], axis=1)
    return both.astype(np.float32).reshape(CORES, HALF, HEAD)


def cos_sin(table):
    first = lax.broadcasted_iota(jnp.int32, table.shape, 1) < HEAD // 2
    turned = swap_halves(table)
    return jnp.where(first, table, turned), jnp.where(first, -turned, table)


def swap_halves(u):
    return pltpu.roll(u, HEAD // 2, 1)


def to_units(keys, values):
    n = keys.shape[0] // PIECE
    return jnp.concatenate(
        [keys.reshape(n, PIECE, HEAD), values.reshape(n, PIECE, HEAD)], axis=1
    )


def from_units(units):
    u = units.astype(f32)
    n = u.shape[0]
    return u[:, :PIECE].reshape(n * PIECE, HEAD), u[:, PIECE:].reshape(n * PIECE, HEAD)


def dot_nn(a, b):
    return lax.dot_general(a, b, (((1,), (0,)), ((), ())), preferred_element_type=f32)


def dot_nt(a, b):
    return lax.dot_general(a, b, (((1,), (1,)), ((), ())), preferred_element_type=f32)


def project_kernel(
    x_ref, wk_ref, wv_ref, gain_ref, table_ref, units_ref, *refs
):
    send_refs, (x_s, w_s, table_s, gain_s, sems, small_sems, send_sems) = refs[:Y - 1], refs[Y - 1:]
    core, y = lax.axis_index("core"), lax.axis_index("y")
    order = [(k, half) for k in range(1, Y) for half in range(X_LO)] + [(0, 0), (0, 1)]
    copies = []
    for n, (k, half) in enumerate(order):
        rows = pl.ds(pl.multiple_of((half * Y + (y ^ k)) * COLS, COLS), COLS)
        copies.append(
            [
                pltpu.make_async_copy(wk_ref.at[rows], w_s.at[n, 0], sems.at[n, 1]),
                pltpu.make_async_copy(wv_ref.at[rows], w_s.at[n, 1], sems.at[n, 2]),
                pltpu.make_async_copy(x_ref.at[:, rows], x_s.at[n], sems.at[n, 0]),
            ]
        )
        for copy in copies[-1]:
            copy.start()
    small = [
        pltpu.make_async_copy(table_ref.at[core], table_s, small_sems.at[0]),
        pltpu.make_async_copy(gain_ref, gain_s, small_sems.at[1]),
    ]
    for copy in small:
        copy.start()
    sends = [
        pltpu.make_async_copy(w_s.at[n], send_refs[k - 1].at[half], send_sems.at[n])
        for n, (k, half) in enumerate(order)
        if k
    ]
    acc = jnp.zeros((HALF, 2 * HEAD), f32)
    for n in range(TENSOR):
        for copy in copies[n]:
            copy.wait()
        if n < len(sends):
            sends[n].start()
        acc += dot_nn(x_s[n], jnp.concatenate([w_s[n, 0], w_s[n, 1]], axis=1))
    for copy in small:
        copy.wait()
    cos, sin = cos_sin(table_s[...])
    raw = acc[:, :HEAD]
    inv = lax.rsqrt(jnp.mean(raw * raw, axis=-1, keepdims=True) + EPS)
    u = raw * inv * gain_s[...]
    keys = u * cos + swap_halves(u) * sin
    high = raw.astype(bf16).astype(f32)
    parts = [keys, acc[:, HEAD:], high, raw - high]
    units_ref[...] = jnp.concatenate(
        [part.reshape(CHIPS, PIECE, HEAD) for part in parts], axis=1
    ).astype(bf16)
    for copy in sends:
        copy.wait()


def project(x, wk, wv, gain, table):
    vmem = pl.BlockSpec(memory_space=pltpu.VMEM)
    hbm = pl.BlockSpec(memory_space=pltpu.HBM)
    anywhere = pl.BlockSpec(memory_space=pl.ANY)
    return pl.pallas_call(
        project_kernel,
        in_specs=[hbm] * 5,
        out_specs=[vmem] + [anywhere] * (Y - 1),
        out_shape=[jax.ShapeDtypeStruct((CHIPS, 2 * UNIT, HEAD), bf16)]
        + [jax.ShapeDtypeStruct((X_LO, 2, COLS, HEAD), bf16)] * (Y - 1),
        scratch_shapes=[
            pltpu.VMEM((TENSOR, HALF, COLS), bf16),
            pltpu.VMEM((TENSOR, 2, COLS, HEAD), bf16),
            pltpu.VMEM((HALF, HEAD), f32),
            pltpu.VMEM((1, HEAD), f32),
            pltpu.SemaphoreType.DMA((TENSOR, 3)),
            pltpu.SemaphoreType.DMA((2,)),
            pltpu.SemaphoreType.DMA((TENSOR - X_LO,)),
        ],
        compiler_params=pltpu.CompilerParams(vmem_limit_bytes=PROJECT_VMEM),
        cost_estimate=pl.CostEstimate(flops=2 * HALF * WIDTH * 256, bytes_accessed=4 << 20, transcendentals=0),
        name="project",
    )(x, wk, wv, gain, table)


def owners(slot_prompt_ref, owner_ref):
    core = lax.axis_index("core")
    prompts = slot_prompt_ref[...]
    row = jnp.zeros_like(prompts)
    for p in range(PROMPTS):
        row = jnp.where(prompts == p, owner_ref[:, p:p + 1], row)
    found = []
    for chip in range(CHIPS):
        first = chip * CORES * R_CAP
        found.append(
            [
                jnp.where(core == 0, row[0, first + r], row[0, first + R_CAP + r])
                for r in range(R_CAP)
            ]
        )
    return found


def select_kernel(slot_prompt_ref, owner_ref, mine_ref, other_ref, out_ref):
    found = owners(slot_prompt_ref, owner_ref)
    for chip in range(CHIPS):
        for r in range(R_CAP):
            q = found[chip][r]
            out_ref[chip, r, 0] = mine_ref[q, :UNIT]
            out_ref[chip, r, 1] = other_ref[q, :UNIT]


def select(slot_prompt, owner, mine, other):
    vmem = pl.BlockSpec(memory_space=pltpu.VMEM)
    return pl.pallas_call(
        select_kernel,
        in_specs=[vmem] * 4,
        out_specs=vmem,
        out_shape=jax.ShapeDtypeStruct((CHIPS, R_CAP, 2, UNIT, HEAD), bf16),
        compiler_params=pltpu.CompilerParams(vmem_limit_bytes=8 << 20),
        name="select",
    )(slot_prompt.reshape(1, -1), owner.reshape(1, -1), mine, other)


def attend_slot(core, length, live, kv_ref, q_ref, g_ref, rk_ref, rv_ref, dq_ref, drk_ref, drv_ref, grads_ref, ds_s, pb_s):
    ka, va = from_units(kv_ref[:, 0])
    kb, vb = from_units(kv_ref[:, 1])
    keys = jnp.concatenate([ka.astype(bf16), kb.astype(bf16), rk_ref[...]], axis=0)
    values = jnp.concatenate([va.astype(bf16), vb.astype(bf16), rv_ref[...]], axis=0)
    row = lax.broadcasted_iota(jnp.int32, (HALF, HEAD), 0)
    column = lax.broadcasted_iota(jnp.int32, (HALF, HEAD), 1)
    hidden = lambda first: jnp.where((column == 0) & (row + first >= length), FAR, 0.0)
    far = jnp.concatenate(
        [
            hidden(core * HALF),
            hidden((1 - core) * HALF),
            jnp.where((column == row) & (row > 0), FAR, 0.0),
        ],
        axis=0,
    ).astype(bf16)
    early = jnp.where((column == 0) | (column > row), 1.0, 0.0).astype(bf16)
    keys_far = jnp.concatenate([keys, far], axis=1)
    for h in range(0, GROUPS, PAIRS):
        cols = slice(h * HEAD, (h + PAIRS) * HEAD)
        stack = lambda ref: jnp.concatenate([ref[:, (h + i) * HEAD:(h + i + 1) * HEAD] for i in range(PAIRS)], axis=0)
        qh = jnp.concatenate([stack(q_ref), jnp.concatenate([early] * PAIRS, axis=0)], axis=1)
        st = dot_nt(keys_far, qh)
        dpt = dot_nt(values, stack(g_ref))
        top = jnp.max(st, axis=0, keepdims=True)
        e = jnp.exp2((st - top) * EXP2_SCALE)
        inv = 1.0 / jnp.sum(e, axis=0, keepdims=True)
        delta = jnp.sum(e * dpt, axis=0, keepdims=True) * inv
        p = e * inv
        pb_s[:, cols] = p.astype(bf16)
        ds_s[:, cols] = (p * (dpt - delta)).astype(bf16)
    rows_of = lambda ref: jnp.concatenate([ref[:, h * HEAD:(h + 1) * HEAD] for h in range(GROUPS)], axis=0)
    keep = jnp.where(live, 1.0, 0.0)
    kept = lambda x: x * keep
    dk = kept(dot_nn(ds_s[...], rows_of(q_ref)) * SCALE)
    dv = kept(dot_nn(pb_s[...], rows_of(g_ref)))
    grads_ref[:, 0] = to_units(dk[:HALF], dv[:HALF]).astype(bf16)
    grads_ref[:, 1] = to_units(dk[HALF:PLEN], dv[HALF:PLEN]).astype(bf16)
    drk_ref[...] = dk[PLEN:].astype(bf16)
    drv_ref[...] = dv[PLEN:].astype(bf16)
    keys_t = keys.T
    for h in range(0, GROUPS, PAIRS):
        d_q = kept(dot_nn(keys_t, ds_s[:, h * HEAD:(h + PAIRS) * HEAD]) * SCALE)
        for i in range(PAIRS):
            dq_ref[:, (h + i) * HEAD:(h + i + 1) * HEAD] = d_q[:, i * HEAD:(i + 1) * HEAD].T.astype(bf16)


def entry(ref, index):
    row = ref[...]
    here = lax.broadcasted_iota(jnp.int32, row.shape, 1) == index
    return jnp.sum(jnp.where(here, row, 0).astype(f32), axis=1, keepdims=True).astype(jnp.int32)


def attend_kernel(
    counts_ref, slot_prompt_ref, lengths_ref,
    kv_ref, q_ref, g_ref, rk_ref, rv_ref,
    dq_ref, drk_ref, drv_ref, grads_ref,
    ds_s, pb_s,
):
    core, dp = lax.axis_index("core"), lax.axis_index(DP)
    for slot in range(R_CAP):
        rows = pl.ds(slot * RLEN, RLEN)
        kv = kv_ref.at[:, slot]
        ins = [r.at[rows] for r in (q_ref, g_ref, rk_ref, rv_ref)]
        outs = [r.at[rows] for r in (dq_ref, drk_ref, drv_ref)] + [grads_ref.at[:, slot]]

        prompt = entry(slot_prompt_ref, dp * R_CAP + slot)
        length = entry(lengths_ref, prompt)
        live = entry(counts_ref, dp) > slot
        attend_slot(core, length, live, kv, *ins, *outs, ds_s.at[slot], pb_s.at[slot])


def attend(counts, slot_prompt, lengths, kv, q, g, rk, rv):
    width = GROUPS * HEAD
    vmem = pl.BlockSpec(memory_space=pltpu.VMEM)
    return pl.pallas_call(
        attend_kernel,
        in_specs=[vmem] * 8,
        out_specs=[vmem] * 4,
        out_shape=[
            jax.ShapeDtypeStruct((R_CAP * RLEN, width), bf16),
            jax.ShapeDtypeStruct((R_CAP * RLEN, HEAD), bf16),
            jax.ShapeDtypeStruct((R_CAP * RLEN, HEAD), bf16),
            jax.ShapeDtypeStruct((CHIPS, R_CAP, 2, UNIT, HEAD), bf16),
        ],
        scratch_shapes=[
            pltpu.VMEM((R_CAP, PLEN + RLEN, width), bf16),
            pltpu.VMEM((R_CAP, PLEN + RLEN, width), bf16),
        ],
        compiler_params=pltpu.CompilerParams(vmem_limit_bytes=16 << 20),
        cost_estimate=pl.CostEstimate(flops=10 * 2 * 384 * 1024 * 128, bytes_accessed=3 << 20, transcendentals=2 * 384 * 1024),
        name="attend",
    )(counts.reshape(1, -1), slot_prompt.reshape(1, -1), lengths.reshape(1, -1), kv, q, g, rk, rv)


def collect_kernel(slot_prompt_ref, owner_ref, got_ref, mine_ref, other_ref, acc):
    found = owners(slot_prompt_ref, owner_ref)
    acc[...] = jnp.zeros_like(acc)
    for chip in range(CHIPS):
        for r in range(R_CAP):
            q = found[chip][r]
            acc[q] += got_ref[chip, r].astype(f32)
    mine_ref[...] = acc[:, 0]
    other_ref[...] = acc[:, 1].astype(bf16)


def collect(slot_prompt, owner, got):
    vmem = pl.BlockSpec(memory_space=pltpu.VMEM)
    return pl.pallas_call(
        collect_kernel,
        in_specs=[vmem] * 3,
        out_specs=[vmem, vmem],
        out_shape=[
            jax.ShapeDtypeStruct((CHIPS, UNIT, HEAD), f32),
            jax.ShapeDtypeStruct((CHIPS, UNIT, HEAD), bf16),
        ],
        scratch_shapes=[pltpu.VMEM((CHIPS, 2, UNIT, HEAD), f32)],
        compiler_params=pltpu.CompilerParams(vmem_limit_bytes=8 << 20),
        name="collect",
    )(slot_prompt.reshape(1, -1), owner.reshape(1, -1), got)


def unkey_kernel(sum_ref, other_ref, units_ref, gain_ref, table_ref, out_ref):
    core, chip = lax.axis_index("core"), lax.axis_index(SPREAD)
    rows = pl.ds(pl.multiple_of(chip * PIECE, PIECE), PIECE)
    cos, sin = cos_sin(table_ref[core, rows])
    total = sum_ref[...] + other_ref[...].astype(f32)
    units = units_ref[...].astype(f32)
    dk, dv = total[:, :PIECE], total[:, PIECE:]
    raw = units[:, UNIT:UNIT + PIECE] + units[:, UNIT + PIECE:]
    inv = lax.rsqrt(jnp.mean(raw * raw, axis=-1, keepdims=True) + EPS)
    turned = swap_halves((dk * sin).reshape(HALF, HEAD)).reshape(CHIPS, PIECE, HEAD)
    dn = (dk * cos + turned) * gain_ref[...]
    dot = jnp.mean(raw * dn, axis=-1, keepdims=True)
    d_raw = inv * (dn - raw * (inv * inv * dot))
    out_ref[...] = jnp.concatenate(
        [d_raw.reshape(HALF, HEAD), dv.reshape(HALF, HEAD)], axis=1
    ).astype(bf16)


def unkey(sums, other, units, gain, table):
    vmem = pl.BlockSpec(memory_space=pltpu.VMEM)
    return pl.pallas_call(
        unkey_kernel,
        in_specs=[vmem] * 5,
        out_specs=vmem,
        out_shape=jax.ShapeDtypeStruct((HALF, 2 * HEAD), bf16),
        compiler_params=pltpu.CompilerParams(vmem_limit_bytes=8 << 20),
        name="unkey",
    )(sums, other, units, gain, table)


def own_share_kernel(wk_ref, wv_ref, grads_ref, out_ref):
    y = lax.axis_index("y")
    for half in range(X_LO):
        rows = pl.ds(pl.multiple_of((half * Y + y) * COLS, COLS), COLS)
        w = jnp.concatenate([wk_ref[rows], wv_ref[rows]], axis=1)
        out_ref[half] = dot_nt(grads_ref[...], w)


def own_share(wk, wv, grads):
    vmem = pl.BlockSpec(memory_space=pltpu.VMEM)
    return pl.pallas_call(
        own_share_kernel,
        in_specs=[vmem] * 3,
        out_specs=vmem,
        out_shape=jax.ShapeDtypeStruct((X_LO, HALF, COLS), f32),
        compiler_params=pltpu.CompilerParams(vmem_limit_bytes=16 << 20),
        name="own_share",
    )(wk, wv, grads)


def input_grad_kernel(own_ref, *refs):
    grads, got, out_ref = refs[:Y - 1], refs[Y - 1:-1], refs[-1]
    for half in range(X_LO):
        total = own_ref[half]
        for k in range(1, Y):
            w = jnp.concatenate([got[k - 1][half, 0], got[k - 1][half, 1]], axis=1)
            total += dot_nt(grads[LAST_FAR.index(k)][...], w)
        out_ref[half] = total.reshape(CHIPS, PIECE, COLS).astype(bf16)


def input_grad(own, grads, got):
    vmem = pl.BlockSpec(memory_space=pltpu.VMEM)
    return pl.pallas_call(
        input_grad_kernel,
        in_specs=[vmem] * (2 * Y - 1),
        out_specs=vmem,
        out_shape=jax.ShapeDtypeStruct((X_LO, CHIPS, PIECE, COLS), bf16),
        compiler_params=pltpu.CompilerParams(vmem_limit_bytes=16 << 20),
        cost_estimate=pl.CostEstimate(flops=2 * HALF * WIDTH * 256, bytes_accessed=4 << 20, transcendentals=0),
        name="input_grad",
    )(own, *grads, *got)


def together(first, second):
    flat, tree = jax.tree.flatten((first, second))
    return jax.tree.unflatten(tree, lax.optimization_barrier(flat))


def swap_y(x, k):
    return lax.ppermute(x, "y", [(i, i ^ k) for i in range(Y)])


def spread(x):
    return lax.all_to_all(x, SPREAD, 0, 0, tiled=True)


def swap_cores(x):
    return lax.ppermute(x, "core", [(0, 1), (1, 0)])


def on_device(
    prompt_x, key_matrix, value_matrix, k_gain, queries, response_keys, response_values,
    output_gradient, response_counts, slot_prompt, prompt_owner, prompt_lengths,
):
    table = rope_table()
    gain = k_gain.reshape(1, HEAD)
    with jax.named_scope("keys_out"):
        units, *send = project(prompt_x, key_matrix, value_matrix, gain, table)
        got = [swap_y(send[k - 1], k) for k in range(1, Y)]
        mine = spread(units)
        needed = select(slot_prompt, prompt_owner, mine, swap_cores(mine))
        needed, (got[0], got[2]) = together(spread(needed), (got[0], got[2]))
    with jax.named_scope("attention"):
        dq, drk, drv, grads = attend(
            response_counts, slot_prompt, prompt_lengths,
            needed, queries, output_gradient, response_keys, response_values,
        )
    with jax.named_scope("grads_back"):
        sums, other = collect(slot_prompt, prompt_owner, spread(grads))
        other, got[1] = together(other, got[1])
        both = unkey(sums, swap_cores(other), mine, gain, table)
        others = [swap_y(both, k) for k in LAST_FAR]
        own = own_share(key_matrix, value_matrix, both)
    with jax.named_scope("input_grad"):
        shares = input_grad(own, others, got)
        shares = shares.reshape(X_LO * CHIPS, PIECE, COLS)
        shares = lax.all_to_all(shares, ("x_lo",) + SPREAD, 0, 0, tiled=True)
        shares = shares.reshape(X_LO, CHIPS, PIECE, COLS).astype(f32)
        d_prompt = jnp.sum(shares, axis=0).reshape(HALF, COLS).astype(bf16)
    return dq, drk, drv, d_prompt


def solution(mesh):
    fine = Mesh(mesh.devices.reshape(2, 8, 2, 2, 4), ("x_hi", "z", "core", "x_lo", "y"))
    dp, tensor = ("x_hi", "z", "core"), ("x_lo", "y")
    both = P(dp, tensor)
    return jax.shard_map(
        on_device,
        mesh=fine,
        in_specs=(P(dp, None), P(None, tensor), P(None, tensor), P(), both, both, both, both, P(), P(), P(), P()),
        out_specs=(both,) * 4,
        check_vma=False,
    )
```
